32 devices in a mesh: fsdp: 16 (over z, x, core), tensor: 2 (over y).
Axes of the slice: x: 2, y: 2, z: 4, core: 2. Of those that a mesh axis runs over, the one named last changes fastest.
Arguments:
- gate_pre: bfloat16 [3072, 14336], P(('fsdp', 'tensor')), may hold values from -6 to 6
- up_pre: bfloat16 [3072, 14336], P(('fsdp', 'tensor')), may hold values from -6 to 6
- cotangent: bfloat16 [3072, 4096], P('fsdp'), may hold values from -6 to 6
- w_slots: bfloat16 [2, 48, 128, 128], P('tensor', 'fsdp'), may hold values from -0.15625 to 0.15625
- slot_ids: int32 [2, 48], P('tensor'), may hold values from -1 to 1791, as said below
Outputs:
- d_gate: bfloat16 [3072, 14336], P(('fsdp', 'tensor'))
- d_up: bfloat16 [3072, 14336], P(('fsdp', 'tensor'))
- w_grad: float32 [2, 48, 128, 128], P('tensor', 'fsdp')
The draws below stay inside these ranges and needn't reach their ends.
Inputs may be any that keep to these rules, and one draw needn't show every extreme that they name: `slot_ids`: in row t, slots s * 3 to s * 3 + 2 list the kept blocks owned by fsdp index s in tensor slice t as local row block * 32 + column block, filling the first slots and -1 in the rest; every owner has 2 or 3 kept blocks, some owner of every row exactly 3 and some exactly 2; no block id appears twice in a row.
All inputs are finite; a program needn't handle non-finite values.
Results may differ from the reference program's by a relative error of at most 0.0085.
Values may be sent and summed in bfloat16 or wider, within the bound.
A program may use at most 128 MiB of HBM per device.

```python
import math
import jax
import jax.numpy as jnp
from jax import lax

D = 4096
FF = 14336
BLOCK = 128
CAP = 3
TOK_DEV = 192
TOKENS = 3072
SLOTS = 48
N_FSDP = 16
N_TENSOR = 2


def draw_slot_ids(key, part):
    block_total = FF // (N_TENSOR * BLOCK) * (D // BLOCK)
    key_list = jax.random.split(jax.random.fold_in(key, 11), N_TENSOR)

    def one_slice(slice_key):
        key_a, key_b, key_c, key_d = jax.random.split(slice_key, 4)
        shuffled = jax.random.permutation(key_a, block_total - 1)[:CAP * N_FSDP].astype(jnp.int32)
        shortfall = (jax.random.randint(key_b, (N_FSDP,), 0, 4) == 0).astype(jnp.int32)
        full_owner = jax.random.randint(key_c, (), 0, N_FSDP)
        short_owner = (full_owner + 1 + jax.random.randint(key_d, (), 0, N_FSDP - 1)) % N_FSDP
        owner_index = jnp.arange(N_FSDP)
        shortfall = jnp.where(owner_index == full_owner, 0, jnp.where(owner_index == short_owner, 1, shortfall))
        slot_index = jnp.arange(CAP * N_FSDP)
        shuffled = jnp.where(slot_index == full_owner * CAP, block_total - 1, shuffled).astype(jnp.int32)
        kept_count = CAP - shortfall
        keep_slot = jnp.arange(CAP)[None, :] < kept_count[:, None]
        return jnp.where(keep_slot, shuffled.reshape(N_FSDP, CAP), -1).reshape(-1)
    return jax.vmap(one_slice)(key_list).astype(jnp.int32)


def block_levels(rng, extent, pieces, smallest, top_value):
    factor_of, own = 1.0, jax.random.fold_in(rng, 6)
    for axis_at, parts in pieces:
        draws = jnp.exp(jax.random.uniform(jax.random.fold_in(own, axis_at), (parts,), jnp.float32, smallest / len(pieces), top_value / len(pieces)))
        factor_of = factor_of * jnp.repeat(draws, extent[axis_at] // parts).reshape([-1 if axis == axis_at else 1 for axis in range(len(extent))])
    return factor_of


def noise(key, shape, deviation, most, shards=(), kind=jnp.bfloat16):
    drawn = jax.random.normal(key, shape, jnp.float32) * deviation
    if len(shards) > 0:
        drawn = block_levels(key, shape, shards, -0.22, 0.18) * drawn
    return jnp.clip(drawn, min=-most, max=most).astype(kind)


def setup_inputs(seed: int = 0) -> dict:
    keys = jax.random.split(jax.random.key(seed), 6)
    gate_pre = noise(keys[0], (TOKENS, FF), 1.0, 6.0, ((0, 32),))
    up_pre = noise(keys[1], (TOKENS, FF), 1.0, 6.0, ((0, 32),))
    cotangent = noise(keys[2], (TOKENS, D), 1.0, 6.0, ((0, 16),))
    w_slots = noise(keys[3], (N_TENSOR, SLOTS, BLOCK, BLOCK), (D * 2 // 5) ** -0.5, 0.15625, ((0, 2), (1, 16)))
    slot_ids = draw_slot_ids(jax.random.fold_in(keys[5], 71), 0)
    return dict(gate_pre=gate_pre, up_pre=up_pre, cotangent=cotangent, w_slots=w_slots, slot_ids=slot_ids)


def reference(gate_pre, up_pre, cotangent, w_slots, slot_ids):
    n_slice = N_TENSOR
    ff_dev = FF // N_TENSOR
    row_count = ff_dev // BLOCK
    col_count = D // BLOCK
    gate_f = gate_pre.astype(jnp.float32)
    up_f = up_pre.astype(jnp.float32)
    gate_sig = jax.nn.sigmoid(gate_f)
    hidden = (gate_f * gate_sig * up_f).astype(jnp.bfloat16)
    usable = slot_ids >= 0
    safe_ids = jnp.maximum(slot_ids, 0)
    row_index = jnp.where(usable, safe_ids // col_count, row_count).astype(jnp.int32)
    col_index = (safe_ids % col_count).astype(jnp.int32)
    row_clip = jnp.minimum(row_index, row_count - 1)
    slice_index = jnp.broadcast_to(jnp.arange(n_slice, dtype=jnp.int32)[:, None], slot_ids.shape)
    flat_rows = (slice_index * row_count + row_clip).reshape(-1)
    onehot = (row_index[:, :, None] == jnp.arange(row_count, dtype=jnp.int32)[None, None, :]).astype(jnp.float32)
    weight_f = w_slots.astype(jnp.float32)
    grad_scale = 1.0 / math.sqrt(TOKENS)
    usable_f = usable.astype(jnp.float32)
    hidden_groups = hidden.reshape(N_FSDP, TOK_DEV, n_slice * row_count, BLOCK)
    cot_groups = cotangent.reshape(N_FSDP, TOK_DEV, col_count, BLOCK)

    def advance(running, packed_item):
        hidden_g, cot_g = packed_item
        dy_picked = jnp.take(cot_g, col_index.reshape(-1), axis=1).reshape(TOK_DEV, n_slice, SLOTS, BLOCK).astype(jnp.float32)
        h_picked = jnp.take(hidden_g, flat_rows, axis=1).reshape(TOK_DEV, n_slice, SLOTS, BLOCK).astype(jnp.float32)
        contrib = jnp.einsum('ktsb,tsab->ktsa', dy_picked, weight_f, precision=lax.Precision.HIGHEST)
        dh_blocks = jnp.einsum('ktsa,tsr->ktra', contrib, onehot, precision=lax.Precision.HIGHEST)
        partial_value = jnp.einsum('ktsa,ktsb->tsab', h_picked, dy_picked, precision=lax.Precision.HIGHEST)
        partial_value = (partial_value * (grad_scale * usable_f)[:, :, None, None]).astype(jnp.bfloat16)
        return (running + partial_value.astype(jnp.float32), dh_blocks)
    start_grad = jnp.zeros((n_slice, SLOTS, BLOCK, BLOCK), jnp.float32)
    w_grad, dh_all = lax.scan(advance, start_grad, (hidden_groups, cot_groups))
    d_hidden = dh_all.reshape(TOKENS, FF).astype(jnp.bfloat16)
    dh_f = d_hidden.astype(jnp.float32)
    d_gate = (dh_f * up_f * (gate_sig * (1.0 + gate_f * (1.0 - gate_sig)))).astype(jnp.bfloat16)
    d_up = (dh_f * (gate_f * gate_sig)).astype(jnp.bfloat16)
    return (d_gate, d_up, w_grad)
```

```python
import functools
import math

import jax
import jax.numpy as jnp
from jax import lax
from jax.experimental import pallas as pl
from jax.experimental.pallas import tpu as pltpu
from jax.sharding import PartitionSpec as P

MIB = 1 << 20


def swiglu_value(gate_part, up_part):
    gate_f = gate_part.astype(jnp.float32)
    gate_sig = jax.nn.sigmoid(gate_f)
    return (gate_f * gate_sig * up_part.astype(jnp.float32)).astype(jnp.bfloat16)


def swiglu_grads(dh_part, gate_part, up_part):
    gate_f = gate_part.astype(jnp.float32)
    up_f = up_part.astype(jnp.float32)
    gate_sig = jax.nn.sigmoid(gate_f)
    dh_f = dh_part.astype(jnp.float32)
    grad_gate = (dh_f * up_f * (gate_sig * (1.0 + gate_f * (1.0 - gate_sig)))).astype(jnp.bfloat16)
    grad_up = (dh_f * (gate_f * gate_sig)).astype(jnp.bfloat16)
    return (grad_gate, grad_up)


def wide_body(gate_pre, up_pre, cotangent, w_slots, slot_ids):
    n_fsdp = lax.axis_size("fsdp")
    block_size = w_slots.shape[2]
    token_count = cotangent.shape[0]
    model_width = cotangent.shape[1]
    col_count = model_width // block_size
    ff_dev = gate_pre.shape[1] // lax.axis_size("tensor")
    row_count = ff_dev // block_size
    slot_total = slot_ids.shape[1]
    cap_local = w_slots.shape[1]
    slot_list = slot_ids[0]
    usable = slot_list >= 0
    safe_ids = jnp.maximum(slot_list, 0)
    row_index = jnp.where(usable, safe_ids // col_count, row_count)
    col_index = safe_ids % col_count
    row_clip = jnp.minimum(row_index, row_count - 1)
    usable_f = usable.astype(jnp.float32)
    row_range = jnp.arange(row_count, dtype=jnp.int32)
    dy_blocks = cotangent.reshape(token_count, col_count, block_size)
    hidden_seq = swiglu_value(gate_pre, up_pre)
    hidden = lax.all_to_all(hidden_seq, "tensor", split_axis=1, concat_axis=0, tiled=True)
    start_sum = jnp.zeros((token_count, row_count, block_size), jnp.float32)
    running = start_sum
    shard_piece = lax.all_gather(w_slots, "fsdp", axis=1, tiled=True)
    slot_count = shard_piece.shape[1]
    sub_size = math.gcd(slot_count, 48)
    rows_part = row_index.reshape(slot_count // sub_size, sub_size)
    cols_part = col_index.reshape(slot_count // sub_size, sub_size)
    weight_part = shard_piece[0].reshape(slot_count // sub_size, sub_size, block_size, block_size)

    def advance(carried, packed_item):
        rows_now, cols_now, weight_now = packed_item
        dy_picked = jnp.take(dy_blocks, cols_now, axis=1)
        contrib = jnp.einsum(
            "tsb,sab->tsa", dy_picked, weight_now, preferred_element_type=jnp.float32
        )
        onehot = (rows_now[:, None] == row_range[None, :]).astype(jnp.float32)
        added = jnp.einsum("tsa,sr->tra", contrib, onehot, precision=lax.Precision.HIGHEST)
        return (carried + added, None)

    running, _ = lax.scan(advance, running, (rows_part, cols_part, weight_part))
    d_hidden = running.reshape(token_count, ff_dev).astype(jnp.bfloat16)
    grad_scale = 1.0 / math.sqrt(token_count * n_fsdp)
    hidden_blocks = hidden.reshape(token_count, row_count, block_size)
    group_size = math.gcd(slot_total, 48)
    group_count = slot_total // group_size

    def partial_group(packed_item):
        rows_now, cols_now, scale_now = packed_item
        h_picked = jnp.take(hidden_blocks, rows_now, axis=1)
        dy_picked = jnp.take(dy_blocks, cols_now, axis=1)
        product = jnp.einsum(
            "tsa,tsb->sab", h_picked, dy_picked, preferred_element_type=jnp.float32
        )
        return (product * scale_now[:, None, None]).astype(jnp.bfloat16)

    partials = lax.map(
        partial_group,
        (
            row_clip.reshape(group_count, group_size),
            col_index.reshape(group_count, group_size),
            (grad_scale * usable_f).reshape(group_count, group_size),
        ),
    )
    partials = partials.reshape(slot_total, block_size, block_size)
    arrived = lax.all_to_all(partials, "fsdp", split_axis=0, concat_axis=0, tiled=True)
    w_grad = (
        arrived.astype(jnp.float32)
        .reshape(n_fsdp, cap_local, block_size, block_size)
        .sum(axis=0)[None]
    )
    dh_seq = lax.all_to_all(d_hidden, "tensor", split_axis=0, concat_axis=1, tiled=True)
    d_gate, d_up = swiglu_grads(dh_seq, gate_pre, up_pre)
    return (d_gate, d_up, w_grad)


def partial_kernel(scale, ids_ref, gate_ref, up_ref, cot_ref, out_ref):
    n_tensor, slots, block, _ = out_ref.shape
    tokens, ff = gate_ref.shape
    rows = ff // block // n_tensor
    cols = cot_ref.shape[1] // block
    base = pl.multiple_of(lax.axis_index("tensor") * tokens, tokens)
    for t in range(n_tensor):

        @pl.loop(0, slots, unroll=8)
        def _(s, t=t):
            slot = ids_ref[t, s]
            safe = jnp.maximum(slot, 0)
            r = pl.multiple_of((safe // cols + t * rows) * block, block)
            c = pl.multiple_of((safe % cols) * block, block)
            h = swiglu_value(gate_ref[:, pl.ds(r, block)], up_ref[:, pl.ds(r, block)])
            dy = cot_ref[pl.ds(base, tokens), pl.ds(c, block)]
            part = lax.dot_general(h, dy, (((0,), (0,)), ((), ())), preferred_element_type=jnp.float32)
            out_ref[t, s] = (part * jnp.where(slot >= 0, scale, 0.0)).astype(out_ref.dtype)


def grads_kernel(ids_ref, w_ref, cot_ref, gate_ref, up_ref, dgate_ref, dup_ref, dh_ref):
    n_tensor, slots, block, _ = w_ref.shape
    steps, tokens, width = dh_ref.shape
    rows = steps * width // block // n_tensor
    cols = cot_ref.shape[1] // block
    per = width // block
    base = pl.multiple_of(lax.axis_index("tensor") * tokens, tokens)
    step = pl.program_id(0)

    @pl.when(step == 0)
    def _():
        dh_ref[...] = jnp.zeros_like(dh_ref)
        for t in range(n_tensor):

            @pl.loop(0, slots, unroll=4)
            def _(s, t=t):
                slot = ids_ref[t, s]
                safe = jnp.maximum(slot, 0)
                r = safe // cols + t * rows
                c = pl.multiple_of((safe % cols) * block, block)
                dy = cot_ref[pl.ds(base, tokens), pl.ds(c, block)]
                add = lax.dot_general(dy, w_ref[t, s], (((1,), (1,)), ((), ())), preferred_element_type=jnp.float32)
                at = (r // per, slice(None), pl.ds(pl.multiple_of(r % per * block, block), block))
                dh_ref[at] += jnp.where(slot >= 0, add, 0.0)

    dh = dh_ref[step].astype(jnp.bfloat16)
    dgate_ref[...], dup_ref[...] = swiglu_grads(dh, gate_ref[...], up_ref[...])


def local_partials(ids, gate, up, cot, scale, block):
    n_tensor, slots = ids.shape
    whole = pl.BlockSpec(memory_space=pltpu.VMEM)
    return pl.pallas_call(
        functools.partial(partial_kernel, scale),
        out_shape=jax.ShapeDtypeStruct((n_tensor, slots, block, block), jnp.bfloat16),
        in_specs=[pl.BlockSpec(memory_space=pltpu.SMEM), whole, whole, whole],
        out_specs=whole,
        compiler_params=pltpu.CompilerParams(vmem_limit_bytes=40 * MIB),
    )(ids, gate, up, cot)


def local_grads(ids, w_all, cot, gate, up):
    tokens, ff = gate.shape
    width = 1024
    steps = ff // width
    whole = pl.BlockSpec(memory_space=pltpu.VMEM)
    tile = pl.BlockSpec((tokens, width), lambda i: (0, i))
    return pl.pallas_call(
        grads_kernel,
        grid=(steps,),
        out_shape=[jax.ShapeDtypeStruct(gate.shape, jnp.bfloat16)] * 2,
        in_specs=[pl.BlockSpec(memory_space=pltpu.SMEM), whole, whole, tile, tile],
        out_specs=[tile, tile],
        scratch_shapes=[pltpu.VMEM((steps, tokens, width), jnp.float32)],
        compiler_params=pltpu.CompilerParams(vmem_limit_bytes=40 * MIB),
    )(ids, w_all, cot, gate, up)


def body(gate_pre, up_pre, cotangent, w_slots, slot_ids):
    n_fsdp = lax.axis_size("fsdp")
    cap, block = w_slots.shape[1:3]
    scale = 1.0 / math.sqrt(cotangent.shape[0] * n_fsdp)
    ids = lax.all_gather(slot_ids, "tensor", axis=0, tiled=True)
    w_all = lax.all_gather(lax.all_gather(w_slots, "fsdp", axis=1, tiled=True), "tensor", axis=0, tiled=True)
    partials = local_partials(ids, gate_pre, up_pre, cotangent, scale, block)
    shares = partials.reshape(2, n_fsdp, cap, block, block).swapaxes(0, 1)
    shares = shares.reshape(2 * n_fsdp, cap, block, block)
    arrived = lax.all_to_all(shares, ("fsdp", "tensor"), split_axis=0, concat_axis=0, tiled=True)
    w_grad = arrived.astype(jnp.float32).sum(axis=0)[None]
    d_gate, d_up = local_grads(ids, w_all, cotangent, gate_pre, up_pre)
    return (d_gate, d_up, w_grad)


def solution(mesh):
    placed = (
        P(("fsdp", "tensor"), None),
        P(("fsdp", "tensor"), None),
        P("fsdp", None),
        P("tensor", "fsdp", None, None),
        P("tensor", None),
    )
    small = mesh.shape["tensor"] == 2 and mesh.shape["fsdp"] == 16
    return jax.shard_map(
        body if small else wide_body,
        mesh=mesh,
        in_specs=placed,
        out_specs=(
            P(("fsdp", "tensor"), None),
            P(("fsdp", "tensor"), None),
            P("tensor", "fsdp", None, None),
        ),
        check_vma=False,
    )
```

```python
import functools
import math

import jax
import jax.numpy as jnp
from jax import lax
from jax.experimental import pallas as pl
from jax.experimental.pallas import tpu as pltpu
from jax.sharding import PartitionSpec as P

MIB = 1 << 20


def swiglu_value(gate_part, up_part):
    gate_f = gate_part.astype(jnp.float32)
    gate_sig = jax.nn.sigmoid(gate_f)
    return (gate_f * gate_sig * up_part.astype(jnp.float32)).astype(jnp.bfloat16)


def swiglu_grads(dh_part, gate_part, up_part):
    gate_f = gate_part.astype(jnp.float32)
    up_f = up_part.astype(jnp.float32)
    gate_sig = jax.nn.sigmoid(gate_f)
    dh_f = dh_part.astype(jnp.float32)
    grad_gate = (dh_f * up_f * (gate_sig * (1.0 + gate_f * (1.0 - gate_sig)))).astype(jnp.bfloat16)
    grad_up = (dh_f * (gate_f * gate_sig)).astype(jnp.bfloat16)
    return (grad_gate, grad_up)


def wide_body(gate_pre, up_pre, cotangent, w_slots, slot_ids):
    n_fsdp = lax.axis_size("fsdp")
    block_size = w_slots.shape[2]
    token_count = cotangent.shape[0]
    model_width = cotangent.shape[1]
    col_count = model_width // block_size
    ff_dev = gate_pre.shape[1] // lax.axis_size("tensor")
    row_count = ff_dev // block_size
    slot_total = slot_ids.shape[1]
    cap_local = w_slots.shape[1]
    slot_list = slot_ids[0]
    usable = slot_list >= 0
    safe_ids = jnp.maximum(slot_list, 0)
    row_index = jnp.where(usable, safe_ids // col_count, row_count)
    col_index = safe_ids % col_count
    row_clip = jnp.minimum(row_index, row_count - 1)
    usable_f = usable.astype(jnp.float32)
    row_range = jnp.arange(row_count, dtype=jnp.int32)
    dy_blocks = cotangent.reshape(token_count, col_count, block_size)
    hidden_seq = swiglu_value(gate_pre, up_pre)
    hidden = lax.all_to_all(hidden_seq, "tensor", split_axis=1, concat_axis=0, tiled=True)
    start_sum = jnp.zeros((token_count, row_count, block_size), jnp.float32)
    running = start_sum
    shard_piece = lax.all_gather(w_slots, "fsdp", axis=1, tiled=True)
    slot_count = shard_piece.shape[1]
    sub_size = math.gcd(slot_count, 48)
    rows_part = row_index.reshape(slot_count // sub_size, sub_size)
    cols_part = col_index.reshape(slot_count // sub_size, sub_size)
    weight_part = shard_piece[0].reshape(slot_count // sub_size, sub_size, block_size, block_size)

    def advance(carried, packed_item):
        rows_now, cols_now, weight_now = packed_item
        dy_picked = jnp.take(dy_blocks, cols_now, axis=1)
        contrib = jnp.einsum(
            "tsb,sab->tsa", dy_picked, weight_now, preferred_element_type=jnp.float32
        )
        onehot = (rows_now[:, None] == row_range[None, :]).astype(jnp.float32)
        added = jnp.einsum("tsa,sr->tra", contrib, onehot, precision=lax.Precision.HIGHEST)
        return (carried + added, None)

    running, _ = lax.scan(advance, running, (rows_part, cols_part, weight_part))
    d_hidden = running.reshape(token_count, ff_dev).astype(jnp.bfloat16)
    grad_scale = 1.0 / math.sqrt(token_count * n_fsdp)
    hidden_blocks = hidden.reshape(token_count, row_count, block_size)
    group_size = math.gcd(slot_total, 48)
    group_count = slot_total // group_size

    def partial_group(packed_item):
        rows_now, cols_now, scale_now = packed_item
        h_picked = jnp.take(hidden_blocks, rows_now, axis=1)
        dy_picked = jnp.take(dy_blocks, cols_now, axis=1)
        product = jnp.einsum(
            "tsa,tsb->sab", h_picked, dy_picked, preferred_element_type=jnp.float32
        )
        return (product * scale_now[:, None, None]).astype(jnp.bfloat16)

    partials = lax.map(
        partial_group,
        (
            row_clip.reshape(group_count, group_size),
            col_index.reshape(group_count, group_size),
            (grad_scale * usable_f).reshape(group_count, group_size),
        ),
    )
    partials = partials.reshape(slot_total, block_size, block_size)
    arrived = lax.all_to_all(partials, "fsdp", split_axis=0, concat_axis=0, tiled=True)
    w_grad = (
        arrived.astype(jnp.float32)
        .reshape(n_fsdp, cap_local, block_size, block_size)
        .sum(axis=0)[None]
    )
    dh_seq = lax.all_to_all(d_hidden, "tensor", split_axis=0, concat_axis=1, tiled=True)
    d_gate, d_up = swiglu_grads(dh_seq, gate_pre, up_pre)
    return (d_gate, d_up, w_grad)


def exchange_kernel(
    scale, ids_ref, ids_vec, gate_hbm, up_hbm, cot_hbm, w_hbm,
    ids_other, con_ref, wgrad_ref,
    ids_in, gate, up, cot, w_all, part, rc, rx0, ry1, ry0, rx1, rz, local, send, recv,
):
    tokens = gate.shape[1]
    cap, block, _ = w_hbm.shape[1:]
    n_z = w_all.shape[3]
    half = block // 2
    cols = cot.shape[0]
    rows = gate.shape[0] // 2
    f = lax.axis_index("fsdp")
    y = lax.axis_index("tensor")
    z, x, k = f // 4, f // 2 % 2, f % 2
    to_core = {"fsdp": f + 1 - 2 * k, "tensor": y}
    to_x = {"fsdp": f + 2 - 4 * x, "tensor": y}
    to_y = {"fsdp": f, "tensor": 1 - y}
    to_z = [{"fsdp": (z + d) % n_z * 4 + x * 2 + k, "tensor": y} for d in range(1, n_z)]
    part_rows = [pl.ds(0, half), pl.ds(half, half)]

    def copy(i, src, dst, to):
        return pltpu.make_async_remote_copy(
            src_ref=src, dst_ref=dst, send_sem=send.at[i], recv_sem=recv.at[i],
            device_id=to, device_id_type=pl.DeviceIdType.MESH,
        )

    def same(i, ref, to):
        return copy(i, ref, ref, to)

    own_w = pltpu.make_async_copy(w_hbm.at[0], w_all.at[k, y, x, z], local.at[3])
    own_w.start()
    own_tokens = pl.ds(pl.multiple_of(y * tokens, tokens), tokens)

    @pl.loop(0, cols)
    def _(i):
        at = pl.ds(pl.multiple_of(i * block, block), block)
        pltpu.make_async_copy(cot_hbm.at[own_tokens, at], cot.at[i], local.at[2]).start()

    @pl.loop(0, 2 * rows)
    def _(i):
        at = pl.ds(pl.multiple_of(i * block, block), block)
        pltpu.make_async_copy(gate_hbm.at[:, at], gate.at[i], local.at[0]).start()
        pltpu.make_async_copy(up_hbm.at[:, at], up.at[i], local.at[1]).start()

    barrier = pltpu.get_barrier_semaphore()
    peers = [to_core, to_x, to_y] + to_z
    for to in peers:
        pl.semaphore_signal(barrier, inc=1, device_id=to, device_id_type=pl.DeviceIdType.MESH)
    pl.semaphore_wait(barrier, len(peers))

    ids_copy = copy(0, ids_vec, ids_in, to_y)
    ids_copy.start()
    ag_z = [copy(1 + d, w_hbm.at[0], w_all.at[k, y, x, z], to_z[d]) for d in range(n_z - 1)]
    for c in ag_z:
        c.start()
    for n, ref in enumerate((gate, up, cot)):
        pltpu.make_async_copy(ref, ref, local.at[n]).wait()
    own_w.wait()

    def partials(core, t, ids):
        @pl.loop(0, 2 * n_z * cap, unroll=8)
        def _(i):
            q, zz, xx = i % cap, i // cap % n_z, i // (cap * n_z)
            slot = ids[0, (zz * 4 + xx * 2 + core) * cap + q]
            safe = lax.max(slot, 0)
            r = lax.div(safe, cols) + t * rows
            c = lax.rem(safe, cols)
            usable = lax.min(slot + 1, 1).astype(jnp.float32)
            h = swiglu_value(gate[r], up[r])
            dy = cot[c]
            got = lax.dot_general(h, dy, (((0,), (0,)), ((), ())), preferred_element_type=jnp.float32)
            part[core, t, xx, zz, q] = (got * (usable * scale)).astype(part.dtype)

    def contribs(core, t, xx, ids):
        @pl.loop(0, n_z * cap, unroll=6)
        def _(i):
            q, zz = i % cap, i // cap
            slot = ids[0, (zz * 4 + xx * 2 + core) * cap + q]
            c = lax.rem(lax.max(slot, 0), cols)
            usable = lax.min(slot + 1, 1).astype(jnp.float32)
            got = lax.dot_general(
                cot[c], w_all[core, t, xx, zz, q], (((1,), (1,)), ((), ())),
                preferred_element_type=jnp.float32,
            )
            con_ref[core, t, xx, zz, q] = (got * usable).astype(con_ref.dtype)

    def add(dst, src):
        total = dst[...].astype(jnp.float32) + src[...].astype(jnp.float32)
        dst[...] = total.astype(dst.dtype)

    partials(1 - k, y, ids_ref)
    core_p = [copy(13, part.at[1 - k, y], rc.at[y], to_core)]
    core_p[0].start()
    ids_copy.wait_recv()
    ids_local = pltpu.make_async_copy(ids_in, ids_other, local.at[4])
    ids_local.start()
    ids_local.wait()
    partials(1 - k, 1 - y, ids_other)
    core_p.append(copy(14, part.at[1 - k, 1 - y], rc.at[1 - y], to_core))
    core_p[1].start()
    partials(k, y, ids_ref)
    partials(k, 1 - y, ids_other)

    for c in ag_z:
        c.wait_recv()
    core_w = [same(4, w_all.at[k, y, x], to_core)]
    ag_x0 = same(5, w_all.at[k, y, x, :, :, part_rows[0]], to_x)
    ag_y1 = same(6, w_all.at[k, y, x, :, :, part_rows[1]], to_y)
    ag_x0.start()
    ag_y1.start()
    core_w[0].start()

    for n, t in enumerate((y, 1 - y)):
        core_p[n].wait_recv()

        @pl.loop(0, 2 * n_z)
        def _(i, t=t):
            at = (t, i // n_z, i % n_z)
            add(part.at[(k,) + at], rc.at[at])

    rs_x0 = copy(15, part.at[k, :, 1 - x, :, :, part_rows[0]], rx0, to_x)
    rs_y1 = copy(16, part.at[k, 1 - y, :, :, :, part_rows[1]], ry1, to_y)
    rs_x0.start()
    rs_y1.start()

    ag_x0.wait_recv()
    ag_y0 = same(9, w_all.at[k, y, :, :, :, part_rows[0]], to_y)
    ag_y0.start()
    core_w.append(same(7, w_all.at[k, y, 1 - x, :, :, part_rows[0]], to_core))
    core_w[1].start()
    ag_y1.wait_recv()
    ag_x1 = same(10, w_all.at[k, :, x, :, :, part_rows[1]], to_x)
    ag_x1.start()
    core_w.append(same(8, w_all.at[k, 1 - y, x, :, :, part_rows[1]], to_core))
    core_w[2].start()

    contribs(k, y, x, ids_ref)
    core_w[0].wait_recv()
    contribs(1 - k, y, x, ids_ref)

    rs_x0.wait_recv()

    @pl.loop(0, 2 * n_z)
    def _(i):
        add(part.at[k, i // n_z, x, i % n_z, :, part_rows[0]], rx0.at[i // n_z, i % n_z])

    rs_y0 = copy(17, part.at[k, 1 - y, x, :, :, part_rows[0]], ry0, to_y)
    rs_y0.start()
    rs_y1.wait_recv()

    @pl.loop(0, 2 * n_z)
    def _(i):
        add(part.at[k, y, i // n_z, i % n_z, :, part_rows[1]], ry1.at[i // n_z, i % n_z])

    rs_x1 = copy(18, part.at[k, y, 1 - x, :, :, part_rows[1]], rx1, to_x)
    rs_x1.start()

    ag_y0.wait_recv()
    core_w.append(same(11, w_all.at[k, 1 - y, :, :, :, part_rows[0]], to_core))
    core_w[3].start()
    ag_x1.wait_recv()
    core_w.append(same(12, w_all.at[k, :, 1 - x, :, :, part_rows[1]], to_core))
    core_w[4].start()

    rs_z = []
    for p, came, into in ((0, rs_y0, ry0), (1, rs_x1, rx1)):
        came.wait_recv()

        @pl.loop(0, n_z)
        def _(i, p=p, into=into):
            add(part.at[k, y, x, i, :, part_rows[p]], into.at[i])

        for d in range(n_z - 1):
            c = copy(19 + p * (n_z - 1) + d, part.at[k, y, x, (z + d + 1) % n_z, :, part_rows[p]], rz.at[d, p], to_z[d])
            c.start()
            rs_z.append(c)

    contribs(k, y, 1 - x, ids_ref)
    contribs(k, 1 - y, x, ids_other)
    contribs(k, 1 - y, 1 - x, ids_other)
    for c in core_w[1:]:
        c.wait_recv()
    contribs(1 - k, y, 1 - x, ids_ref)
    contribs(1 - k, 1 - y, x, ids_other)
    contribs(1 - k, 1 - y, 1 - x, ids_other)

    for c in rs_z:
        c.wait_recv()
    for p in range(2):
        total = part[k, y, x, z, :, part_rows[p]].astype(jnp.float32)
        for d in range(n_z - 1):
            total = total + rz[d, p].astype(jnp.float32)
        wgrad_ref[0, :, part_rows[p]] = total
    for c in [ids_copy, ag_x0, ag_y1, ag_y0, ag_x1, rs_x0, rs_y1, rs_y0, rs_x1] + ag_z + core_p + core_w + rs_z:
        c.wait_send()


def exchange(gate, up, cot, w, ids, scale):
    tokens, ff = gate.shape
    cap, block = w.shape[1:3]
    bf16 = jnp.bfloat16
    any_spec = pl.BlockSpec(memory_space=pl.ANY)
    smem = pl.BlockSpec(memory_space=pltpu.SMEM)
    whole = pl.BlockSpec(memory_space=pltpu.VMEM)
    n_z = lax.axis_size("fsdp") // 4
    half = block // 2
    return pl.pallas_call(
        functools.partial(exchange_kernel, scale),
        out_shape=[
            jax.ShapeDtypeStruct(ids.shape, ids.dtype),
            jax.ShapeDtypeStruct((2, 2, 2, n_z, cap, tokens, block), bf16),
            jax.ShapeDtypeStruct(w.shape, jnp.float32),
        ],
        in_specs=[smem, whole, any_spec, any_spec, any_spec, any_spec],
        out_specs=[smem, whole, whole],
        scratch_shapes=[
            pltpu.VMEM(ids.shape, ids.dtype),
            pltpu.VMEM((ff // block, tokens, block), bf16),
            pltpu.VMEM((ff // block, tokens, block), bf16),
            pltpu.VMEM((cot.shape[1] // block, tokens, block), bf16),
            pltpu.VMEM((2, 2, 2, n_z, cap, block, block), bf16),
            pltpu.VMEM((2, 2, 2, n_z, cap, block, block), bf16),
            pltpu.VMEM((2, 2, n_z, cap, block, block), bf16),
            pltpu.VMEM((2, n_z, cap, half, block), bf16),
            pltpu.VMEM((2, n_z, cap, half, block), bf16),
            pltpu.VMEM((n_z, cap, half, block), bf16),
            pltpu.VMEM((n_z, cap, half, block), bf16),
            pltpu.VMEM((n_z - 1, 2, cap, half, block), bf16),
            pltpu.SemaphoreType.DMA((5,)),
            pltpu.SemaphoreType.DMA((19 + 2 * (n_z - 1),)),
            pltpu.SemaphoreType.DMA((19 + 2 * (n_z - 1),)),
        ],
        compiler_params=pltpu.CompilerParams(
            collective_id=0, has_side_effects=True, vmem_limit_bytes=48 * MIB
        ),
    )(ids, ids, gate, up, cot, w)


def grads_kernel(cols, ids_ref, other_ref, con_ref, gate_ref, up_ref, dgate_ref, dup_ref, dh_ref):
    n_z, cap, tokens, block = con_ref.shape[3:]
    steps, _, width = dh_ref.shape
    per = width // block
    rows = steps * per // 2
    y = lax.axis_index("tensor")
    step = pl.program_id(0)

    @pl.when(step == 0)
    def _():
        dh_ref[...] = jnp.zeros_like(dh_ref)
        for t, ids in ((y, ids_ref), (1 - y, other_ref)):

            @pl.loop(0, 4 * n_z * cap, unroll=4)
            def _(s, t=t, ids=ids):
                slot = ids[0, s]
                f = s // cap
                r = jnp.maximum(slot, 0) // cols + t * rows
                at = (r // per, slice(None), pl.ds(pl.multiple_of(r % per * block, block), block))
                dh_ref[at] += con_ref[f % 2, t, f // 2 % 2, f // 4, s % cap].astype(jnp.float32)

    dh = dh_ref[step].astype(jnp.bfloat16)
    dgate_ref[...], dup_ref[...] = swiglu_grads(dh, gate_ref[...], up_ref[...])


def local_grads(ids, other, contrib, cols, gate, up):
    tokens, ff = gate.shape
    width = 1024
    steps = ff // width
    smem = pl.BlockSpec(memory_space=pltpu.SMEM)
    tile = pl.BlockSpec((tokens, width), lambda i: (0, i))
    return pl.pallas_call(
        functools.partial(grads_kernel, cols),
        grid=(steps,),
        out_shape=[jax.ShapeDtypeStruct(gate.shape, jnp.bfloat16)] * 2,
        in_specs=[smem, smem, pl.BlockSpec(memory_space=pltpu.VMEM), tile, tile],
        out_specs=[tile, tile],
        scratch_shapes=[pltpu.VMEM((steps, tokens, width), jnp.float32)],
        compiler_params=pltpu.CompilerParams(vmem_limit_bytes=40 * MIB),
    )(ids, other, contrib, gate, up)


def body(gate_pre, up_pre, cotangent, w_slots, slot_ids):
    scale = 1.0 / math.sqrt(cotangent.shape[0] * lax.axis_size("fsdp"))
    other, contrib, w_grad = exchange(gate_pre, up_pre, cotangent, w_slots, slot_ids, scale)
    cols = cotangent.shape[1] // w_slots.shape[2]
    d_gate, d_up = local_grads(slot_ids, other, contrib, cols, gate_pre, up_pre)
    return (d_gate, d_up, w_grad)


def solution(mesh):
    placed = (
        P(("fsdp", "tensor"), None),
        P(("fsdp", "tensor"), None),
        P("fsdp", None),
        P("tensor", "fsdp", None, None),
        P("tensor", None),
    )
    small = mesh.shape["tensor"] == 2 and mesh.shape["fsdp"] == 16
    return jax.shard_map(
        body if small else wide_body,
        mesh=mesh,
        in_specs=placed,
        out_specs=(
            P(("fsdp", "tensor"), None),
            P(("fsdp", "tensor"), None),
            P("tensor", "fsdp", None, None),
        ),
        check_vma=False,
    )
```

```python
import functools
import math

import jax
import jax.numpy as jnp
from jax import lax
from jax.experimental import pallas as pl
from jax.experimental.pallas import tpu as pltpu
from jax.sharding import PartitionSpec as P

MIB = 1 << 20


def swiglu_value(gate_part, up_part):
    gate_f = gate_part.astype(jnp.float32)
    gate_sig = jax.nn.sigmoid(gate_f)
    return (gate_f * gate_sig * up_part.astype(jnp.float32)).astype(jnp.bfloat16)


def swiglu_grads(dh_part, gate_part, up_part):
    gate_f = gate_part.astype(jnp.float32)
    up_f = up_part.astype(jnp.float32)
    gate_sig = jax.nn.sigmoid(gate_f)
    dh_f = dh_part.astype(jnp.float32)
    grad_gate = (dh_f * up_f * (gate_sig * (1.0 + gate_f * (1.0 - gate_sig)))).astype(jnp.bfloat16)
    grad_up = (dh_f * (gate_f * gate_sig)).astype(jnp.bfloat16)
    return (grad_gate, grad_up)


def wide_body(gate_pre, up_pre, cotangent, w_slots, slot_ids):
    n_fsdp = lax.axis_size("fsdp")
    block_size = w_slots.shape[2]
    token_count = cotangent.shape[0]
    model_width = cotangent.shape[1]
    col_count = model_width // block_size
    ff_dev = gate_pre.shape[1] // lax.axis_size("tensor")
    row_count = ff_dev // block_size
    slot_total = slot_ids.shape[1]
    cap_local = w_slots.shape[1]
    slot_list = slot_ids[0]
    usable = slot_list >= 0
    safe_ids = jnp.maximum(slot_list, 0)
    row_index = jnp.where(usable, safe_ids // col_count, row_count)
    col_index = safe_ids % col_count
    row_clip = jnp.minimum(row_index, row_count - 1)
    usable_f = usable.astype(jnp.float32)
    row_range = jnp.arange(row_count, dtype=jnp.int32)
    dy_blocks = cotangent.reshape(token_count, col_count, block_size)
    hidden_seq = swiglu_value(gate_pre, up_pre)
    hidden = lax.all_to_all(hidden_seq, "tensor", split_axis=1, concat_axis=0, tiled=True)
    start_sum = jnp.zeros((token_count, row_count, block_size), jnp.float32)
    running = start_sum
    shard_piece = lax.all_gather(w_slots, "fsdp", axis=1, tiled=True)
    slot_count = shard_piece.shape[1]
    sub_size = math.gcd(slot_count, 48)
    rows_part = row_index.reshape(slot_count // sub_size, sub_size)
    cols_part = col_index.reshape(slot_count // sub_size, sub_size)
    weight_part = shard_piece[0].reshape(slot_count // sub_size, sub_size, block_size, block_size)

    def advance(carried, packed_item):
        rows_now, cols_now, weight_now = packed_item
        dy_picked = jnp.take(dy_blocks, cols_now, axis=1)
        contrib = jnp.einsum(
            "tsb,sab->tsa", dy_picked, weight_now, preferred_element_type=jnp.float32
        )
        onehot = (rows_now[:, None] == row_range[None, :]).astype(jnp.float32)
        added = jnp.einsum("tsa,sr->tra", contrib, onehot, precision=lax.Precision.HIGHEST)
        return (carried + added, None)

    running, _ = lax.scan(advance, running, (rows_part, cols_part, weight_part))
    d_hidden = running.reshape(token_count, ff_dev).astype(jnp.bfloat16)
    grad_scale = 1.0 / math.sqrt(token_count * n_fsdp)
    hidden_blocks = hidden.reshape(token_count, row_count, block_size)
    group_size = math.gcd(slot_total, 48)
    group_count = slot_total // group_size

    def partial_group(packed_item):
        rows_now, cols_now, scale_now = packed_item
        h_picked = jnp.take(hidden_blocks, rows_now, axis=1)
        dy_picked = jnp.take(dy_blocks, cols_now, axis=1)
        product = jnp.einsum(
            "tsa,tsb->sab", h_picked, dy_picked, preferred_element_type=jnp.float32
        )
        return (product * scale_now[:, None, None]).astype(jnp.bfloat16)

    partials = lax.map(
        partial_group,
        (
            row_clip.reshape(group_count, group_size),
            col_index.reshape(group_count, group_size),
            (grad_scale * usable_f).reshape(group_count, group_size),
        ),
    )
    partials = partials.reshape(slot_total, block_size, block_size)
    arrived = lax.all_to_all(partials, "fsdp", split_axis=0, concat_axis=0, tiled=True)
    w_grad = (
        arrived.astype(jnp.float32)
        .reshape(n_fsdp, cap_local, block_size, block_size)
        .sum(axis=0)[None]
    )
    dh_seq = lax.all_to_all(d_hidden, "tensor", split_axis=0, concat_axis=1, tiled=True)
    d_gate, d_up = swiglu_grads(dh_seq, gate_pre, up_pre)
    return (d_gate, d_up, w_grad)


def sigmoid(value):
    return 0.5 + 0.5 * jnp.tanh(0.5 * value)


def hidden_value(gate_part, up_part):
    gate_f = gate_part.astype(jnp.float32)
    return (gate_f * sigmoid(gate_f) * up_part.astype(jnp.float32)).astype(jnp.bfloat16)


def exchange_kernel(
    scale, ids_ref, ids_vec, gate_hbm, up_hbm, cot_hbm, w_hbm,
    ids_other, con_ref, wgrad_ref,
    ids_in, gate, up, cot, w_all, part, rc, rx0, ry1, ry0, rx1, rz, local, send, recv,
):
    tokens = gate.shape[1]
    cap, block, _ = w_hbm.shape[1:]
    n_z = w_all.shape[3]
    half = block // 2
    cols = cot.shape[0]
    rows = gate.shape[0] // 2
    f = lax.axis_index("fsdp")
    y = lax.axis_index("tensor")
    z, x, k = f // 4, f // 2 % 2, f % 2
    to_core = {"fsdp": f + 1 - 2 * k, "tensor": y}
    to_x = {"fsdp": f + 2 - 4 * x, "tensor": y}
    to_y = {"fsdp": f, "tensor": 1 - y}
    to_z = [{"fsdp": (z + d) % n_z * 4 + x * 2 + k, "tensor": y} for d in range(1, n_z)]
    part_rows = [pl.ds(0, half), pl.ds(half, half)]

    def copy(i, src, dst, to):
        return pltpu.make_async_remote_copy(
            src_ref=src, dst_ref=dst, send_sem=send.at[i], recv_sem=recv.at[i],
            device_id=to, device_id_type=pl.DeviceIdType.MESH,
        )

    def same(i, ref, to):
        return copy(i, ref, ref, to)

    barrier = pltpu.get_barrier_semaphore()
    peers = [to_core, to_x, to_y] + to_z
    for to in peers:
        pl.semaphore_signal(barrier, inc=1, device_id=to, device_id_type=pl.DeviceIdType.MESH)
    own_tokens = pl.ds(pl.multiple_of(y * tokens, tokens), tokens)

    @pl.loop(0, cols, unroll=4)
    def _(i):
        at = pl.ds(pl.multiple_of(i * block, block), block)
        pltpu.make_async_copy(cot_hbm.at[own_tokens, at], cot.at[i], local.at[2]).start()

    own_w = pltpu.make_async_copy(w_hbm.at[0], w_all.at[k, y, x, z], local.at[3])
    own_w.start()
    pl.semaphore_wait(barrier, len(peers))

    ids_copy = copy(0, ids_vec, ids_in, to_y)
    ids_copy.start()
    ag_x0 = copy(5, w_hbm.at[0, :, part_rows[0]], w_all.at[k, y, x, z, :, part_rows[0]], to_x)
    ag_y1 = copy(6, w_hbm.at[0, :, part_rows[1]], w_all.at[k, y, x, z, :, part_rows[1]], to_y)
    ag_x0.start()
    ag_y1.start()
    ag_z = [copy(1 + d, w_hbm.at[0], w_all.at[k, y, x, z], to_z[d]) for d in range(n_z - 1)]
    for c in ag_z:
        c.start()

    @pl.loop(0, 2 * rows, unroll=4)
    def _(i):
        at = pl.ds(pl.multiple_of(i * block, block), block)
        pltpu.make_async_copy(gate_hbm.at[:, at], gate.at[i], local.at[0]).start()
        pltpu.make_async_copy(up_hbm.at[:, at], up.at[i], local.at[1]).start()

    own_w.wait()
    ids_copy.wait_recv()
    ids_local = pltpu.make_async_copy(ids_in, ids_other, local.at[4])
    ids_local.start()
    ids_local.wait()
    ag_x0.wait_recv()
    ag_zx = [same(23 + d, w_all.at[k, y, 1 - x, z, :, part_rows[0]], to_z[d]) for d in range(n_z - 1)]
    ag_y1.wait_recv()
    ag_zy = [
        same(23 + n_z - 1 + d, w_all.at[k, 1 - y, x, z, :, part_rows[1]], to_z[d]) for d in range(n_z - 1)
    ]
    for c in ag_zx + ag_zy:
        c.start()
    for n, ref in enumerate((gate, up, cot)):
        pltpu.make_async_copy(ref, ref, local.at[n]).wait()

    def partials(core, t, xx, ids):
        @pl.loop(0, n_z * cap, unroll=6)
        def _(i):
            q, zz = i % cap, i // cap
            slot = ids[0, (zz * 4 + xx * 2 + core) * cap + q]
            safe = lax.max(slot, 0)
            r = lax.div(safe, cols) + t * rows
            c = lax.rem(safe, cols)
            usable = lax.min(slot + 1, 1).astype(jnp.float32)
            h = hidden_value(gate[r], up[r])
            dy = cot[c]
            got = lax.dot_general(h, dy, (((0,), (0,)), ((), ())), preferred_element_type=jnp.float32)
            part[core, t, xx, zz, q] = (got * (usable * scale)).astype(part.dtype)

    def contribs(core, t, xx, ids):
        @pl.loop(0, n_z * cap, unroll=6)
        def _(i):
            q, zz = i % cap, i // cap
            slot = ids[0, (zz * 4 + xx * 2 + core) * cap + q]
            c = lax.rem(lax.max(slot, 0), cols)
            usable = lax.min(slot + 1, 1).astype(jnp.float32)
            got = lax.dot_general(
                cot[c], w_all[core, t, xx, zz, q], (((1,), (1,)), ((), ())),
                preferred_element_type=jnp.float32,
            )
            con_ref[core, t, xx, zz, q] = (got * usable).astype(con_ref.dtype)

    def add(dst, src):
        total = dst[...].astype(jnp.float32) + src[...].astype(jnp.float32)
        dst[...] = total.astype(dst.dtype)

    quads = ((1 - y, 1 - x, ids_other), (y, 1 - x, ids_ref), (1 - y, x, ids_other), (y, x, ids_ref))
    core_p = []

    def send_core(n):
        t, xx, ids = quads[n]
        partials(1 - k, t, xx, ids)
        core_p.append(copy(10 + n, part.at[1 - k, t, xx], rc.at[t, xx], to_core))
        core_p[n].start()

    def add_core(n):
        t, xx, _ = quads[n]
        core_p[n].wait_recv()

        @pl.loop(0, n_z)
        def _(i):
            add(part.at[k, t, xx, i], rc.at[t, xx, i])

    def own_core(n):
        t, xx, ids = quads[n]
        partials(k, t, xx, ids)

    send_core(0)
    own_core(0)
    send_core(1)
    add_core(0)
    far = part.at[k, 1 - y, 1 - x]
    rs_xa = copy(14, far.at[:, :, part_rows[0]], rx0.at[1 - y], to_x)
    rs_ya = copy(15, far.at[:, :, part_rows[1]], ry1.at[1 - x], to_y)
    rs_xa.start()
    rs_ya.start()
    own_core(1)
    send_core(2)
    add_core(1)
    rs_xb = copy(16, part.at[k, y, 1 - x, :, :, part_rows[0]], rx0.at[y], to_x)
    rs_xb.start()
    own_core(2)
    send_core(3)
    add_core(2)
    rs_yb = copy(17, part.at[k, 1 - y, x, :, :, part_rows[1]], ry1.at[x], to_y)
    rs_yb.start()
    own_core(3)

    for c in ag_z:
        c.wait_recv()
    mine = w_all.at[k, y, x]
    ag_ya = same(4, mine.at[:, :, part_rows[0]], to_y)
    ag_xa = same(7, mine.at[:, :, part_rows[1]], to_x)
    ag_ya.start()
    ag_xa.start()
    core_w = [same(29, mine, to_core)]
    core_w[0].start()
    add_core(3)

    rs_xa.wait_recv()

    @pl.loop(0, n_z)
    def _(i):
        add(part.at[k, 1 - y, x, i, :, part_rows[0]], rx0.at[1 - y, i])

    rs_y0 = copy(18, part.at[k, 1 - y, x, :, :, part_rows[0]], ry0, to_y)
    rs_y0.start()
    rs_ya.wait_recv()

    @pl.loop(0, n_z)
    def _(i):
        add(part.at[k, y, 1 - x, i, :, part_rows[1]], ry1.at[1 - x, i])

    rs_x1 = copy(19, part.at[k, y, 1 - x, :, :, part_rows[1]], rx1, to_x)
    rs_x1.start()

    def to_core_w(ref):
        core_w.append(same(29 + len(core_w), ref, to_core))
        core_w[-1].start()

    contribs(k, y, x, ids_ref)
    for c in ag_zx:
        c.wait_recv()
    ag_yb = same(8, w_all.at[k, y, 1 - x, :, :, part_rows[0]], to_y)
    ag_yb.start()
    to_core_w(w_all.at[k, y, 1 - x, :, :, part_rows[0]])
    for c in ag_zy:
        c.wait_recv()
    ag_xb = same(9, w_all.at[k, 1 - y, x, :, :, part_rows[1]], to_x)
    ag_xb.start()
    to_core_w(w_all.at[k, 1 - y, x, :, :, part_rows[1]])

    rs_z = []

    def send_z(p, last, into, came, came_into):
        last.wait_recv()
        came.wait_recv()

        @pl.loop(0, n_z)
        def _(i):
            ref = part.at[k, y, x, i, :, part_rows[p]]
            total = ref[...].astype(jnp.float32) + into[i].astype(jnp.float32)
            ref[...] = (total + came_into[i].astype(jnp.float32)).astype(ref.dtype)

        for d in range(n_z - 1):
            src = part.at[k, y, x, (z + d + 1) % n_z, :, part_rows[p]]
            c = copy(37 + p * (n_z - 1) + d, src, rz.at[d, p], to_z[d])
            c.start()
            rs_z.append(c)

    send_z(0, rs_xb, rx0.at[y], rs_y0, ry0)
    send_z(1, rs_yb, ry1.at[x], rs_x1, rx1)

    core_w[0].wait_recv()
    contribs(1 - k, y, x, ids_ref)
    ag_ya.wait_recv()
    to_core_w(w_all.at[k, 1 - y, x, :, :, part_rows[0]])
    contribs(k, 1 - y, x, ids_other)
    ag_xa.wait_recv()
    to_core_w(w_all.at[k, y, 1 - x, :, :, part_rows[1]])
    contribs(k, y, 1 - x, ids_ref)
    for c in (core_w[2], core_w[3]):
        c.wait_recv()
    contribs(1 - k, 1 - y, x, ids_other)
    for c in (core_w[1], core_w[4]):
        c.wait_recv()
    contribs(1 - k, y, 1 - x, ids_ref)
    ag_yb.wait_recv()
    to_core_w(w_all.at[k, 1 - y, 1 - x, :, :, part_rows[0]])
    ag_xb.wait_recv()
    to_core_w(w_all.at[k, 1 - y, 1 - x, :, :, part_rows[1]])
    contribs(k, 1 - y, 1 - x, ids_other)

    for c in rs_z:
        c.wait_recv()
    for p in range(2):
        total = part[k, y, x, z, :, part_rows[p]].astype(jnp.float32)
        for d in range(n_z - 1):
            total = total + rz[d, p].astype(jnp.float32)
        wgrad_ref[0, :, part_rows[p]] = total
    for c in core_w[5:]:
        c.wait_recv()
    contribs(1 - k, 1 - y, 1 - x, ids_other)
    sent = [ids_copy, ag_x0, ag_y1, ag_xa, ag_ya, ag_xb, ag_yb, rs_xa, rs_ya, rs_xb, rs_yb, rs_x1, rs_y0]
    for c in sent + ag_z + ag_zx + ag_zy + core_p + core_w + rs_z:
        c.wait_send()


def exchange(gate, up, cot, w, ids, scale):
    tokens, ff = gate.shape
    cap, block = w.shape[1:3]
    bf16 = jnp.bfloat16
    any_spec = pl.BlockSpec(memory_space=pltpu.HBM)
    smem = pl.BlockSpec(memory_space=pltpu.SMEM)
    whole = pl.BlockSpec(memory_space=pltpu.VMEM)
    n_z = lax.axis_size("fsdp") // 4
    half = block // 2
    return pl.pallas_call(
        functools.partial(exchange_kernel, scale),
        out_shape=[
            jax.ShapeDtypeStruct(ids.shape, ids.dtype),
            jax.ShapeDtypeStruct((2, 2, 2, n_z, cap, tokens, block), bf16),
            jax.ShapeDtypeStruct(w.shape, jnp.float32),
        ],
        in_specs=[smem, whole, any_spec, any_spec, any_spec, any_spec],
        out_specs=[smem, whole, whole],
        scratch_shapes=[
            pltpu.VMEM(ids.shape, ids.dtype),
            pltpu.VMEM((ff // block, tokens, block), bf16),
            pltpu.VMEM((ff // block, tokens, block), bf16),
            pltpu.VMEM((cot.shape[1] // block, tokens, block), bf16),
            pltpu.VMEM((2, 2, 2, n_z, cap, block, block), bf16),
            pltpu.VMEM((2, 2, 2, n_z, cap, block, block), bf16),
            pltpu.VMEM((2, 2, n_z, cap, block, block), bf16),
            pltpu.VMEM((2, n_z, cap, half, block), bf16),
            pltpu.VMEM((2, n_z, cap, half, block), bf16),
            pltpu.VMEM((n_z, cap, half, block), bf16),
            pltpu.VMEM((n_z, cap, half, block), bf16),
            pltpu.VMEM((n_z - 1, 2, cap, half, block), bf16),
            pltpu.SemaphoreType.DMA((5,)),
            pltpu.SemaphoreType.DMA((37 + 2 * (n_z - 1),)),
            pltpu.SemaphoreType.DMA((37 + 2 * (n_z - 1),)),
        ],
        compiler_params=pltpu.CompilerParams(
            collective_id=0, has_side_effects=True, vmem_limit_bytes=48 * MIB
        ),
    )(ids, ids, gate, up, cot, w)


def grads_kernel(cols, ids_ref, other_ref, con_ref, gate_ref, up_ref, dgate_ref, dup_ref, dh_ref):
    n_z, cap, tokens, block = con_ref.shape[3:]
    steps, _, width = dh_ref.shape
    per = width // block
    rows = steps * per // 2
    y = lax.axis_index("tensor")
    step = pl.program_id(0)

    @pl.when(step == 0)
    def _():
        dh_ref[...] = jnp.zeros_like(dh_ref)
        for t, ids in ((y, ids_ref), (1 - y, other_ref)):

            @pl.loop(0, 4 * n_z * cap, unroll=4)
            def _(s, t=t, ids=ids):
                slot = ids[0, s]
                f = s // cap
                r = jnp.maximum(slot, 0) // cols + t * rows
                at = (r // per, slice(None), pl.ds(pl.multiple_of(r % per * block, block), block))
                dh_ref[at] += con_ref[f % 2, t, f // 2 % 2, f // 4, s % cap].astype(jnp.float32)

    gate_f = gate_ref[...].astype(jnp.float32)
    dh = dh_ref[step]
    sig = sigmoid(gate_f)
    silu = gate_f * sig
    dup_ref[...] = (dh * silu).astype(dup_ref.dtype)
    slope = sig + silu * (1.0 - sig)
    dgate_ref[...] = (dh * up_ref[...].astype(jnp.float32) * slope).astype(dgate_ref.dtype)


def local_grads(ids, other, contrib, cols, gate, up):
    tokens, ff = gate.shape
    steps = 8
    width = ff // steps
    smem = pl.BlockSpec(memory_space=pltpu.SMEM)
    tile = pl.BlockSpec((tokens, width), lambda i: (0, i))
    return pl.pallas_call(
        functools.partial(grads_kernel, cols),
        grid=(steps,),
        out_shape=[jax.ShapeDtypeStruct(gate.shape, jnp.bfloat16)] * 2,
        in_specs=[smem, smem, pl.BlockSpec(memory_space=pltpu.VMEM), tile, tile],
        out_specs=[tile, tile],
        scratch_shapes=[pltpu.VMEM((steps, tokens, width), jnp.float32)],
        compiler_params=pltpu.CompilerParams(vmem_limit_bytes=40 * MIB),
    )(ids, other, contrib, gate, up)


def body(gate_pre, up_pre, cotangent, w_slots, slot_ids):
    scale = 1.0 / math.sqrt(cotangent.shape[0] * lax.axis_size("fsdp"))
    other, contrib, w_grad = exchange(gate_pre, up_pre, cotangent, w_slots, slot_ids, scale)
    cols = cotangent.shape[1] // w_slots.shape[2]
    d_gate, d_up = local_grads(slot_ids, other, contrib, cols, gate_pre, up_pre)
    return (d_gate, d_up, w_grad)


def solution(mesh):
    placed = (
        P(("fsdp", "tensor"), None),
        P(("fsdp", "tensor"), None),
        P("fsdp", None),
        P("tensor", "fsdp", None, None),
        P("tensor", None),
    )
    small = mesh.shape["tensor"] == 2 and mesh.shape["fsdp"] == 16
    return jax.shard_map(
        body if small else wide_body,
        mesh=mesh,
        in_specs=placed,
        out_specs=(
            P(("fsdp", "tensor"), None),
            P(("fsdp", "tensor"), None),
            P("tensor", "fsdp", None, None),
        ),
        check_vma=False,
    )
```

```python
import functools
import math

import jax
import jax.numpy as jnp
from jax import lax
from jax.experimental import pallas as pl
from jax.experimental.pallas import tpu as pltpu
from jax.sharding import PartitionSpec as P

MIB = 1 << 20


def swiglu_value(gate_part, up_part):
    gate_f = gate_part.astype(jnp.float32)
    gate_sig = jax.nn.sigmoid(gate_f)
    return (gate_f * gate_sig * up_part.astype(jnp.float32)).astype(jnp.bfloat16)


def swiglu_grads(dh_part, gate_part, up_part):
    gate_f = gate_part.astype(jnp.float32)
    up_f = up_part.astype(jnp.float32)
    gate_sig = jax.nn.sigmoid(gate_f)
    dh_f = dh_part.astype(jnp.float32)
    grad_gate = (dh_f * up_f * (gate_sig * (1.0 + gate_f * (1.0 - gate_sig)))).astype(jnp.bfloat16)
    grad_up = (dh_f * (gate_f * gate_sig)).astype(jnp.bfloat16)
    return (grad_gate, grad_up)


def wide_body(gate_pre, up_pre, cotangent, w_slots, slot_ids):
    n_fsdp = lax.axis_size("fsdp")
    block_size = w_slots.shape[2]
    token_count = cotangent.shape[0]
    model_width = cotangent.shape[1]
    col_count = model_width // block_size
    ff_dev = gate_pre.shape[1] // lax.axis_size("tensor")
    row_count = ff_dev // block_size
    slot_total = slot_ids.shape[1]
    cap_local = w_slots.shape[1]
    slot_list = slot_ids[0]
    usable = slot_list >= 0
    safe_ids = jnp.maximum(slot_list, 0)
    row_index = jnp.where(usable, safe_ids // col_count, row_count)
    col_index = safe_ids % col_count
    row_clip = jnp.minimum(row_index, row_count - 1)
    usable_f = usable.astype(jnp.float32)
    row_range = jnp.arange(row_count, dtype=jnp.int32)
    dy_blocks = cotangent.reshape(token_count, col_count, block_size)
    hidden_seq = swiglu_value(gate_pre, up_pre)
    hidden = lax.all_to_all(hidden_seq, "tensor", split_axis=1, concat_axis=0, tiled=True)
    start_sum = jnp.zeros((token_count, row_count, block_size), jnp.float32)
    running = start_sum
    shard_piece = lax.all_gather(w_slots, "fsdp", axis=1, tiled=True)
    slot_count = shard_piece.shape[1]
    sub_size = math.gcd(slot_count, 48)
    rows_part = row_index.reshape(slot_count // sub_size, sub_size)
    cols_part = col_index.reshape(slot_count // sub_size, sub_size)
    weight_part = shard_piece[0].reshape(slot_count // sub_size, sub_size, block_size, block_size)

    def advance(carried, packed_item):
        rows_now, cols_now, weight_now = packed_item
        dy_picked = jnp.take(dy_blocks, cols_now, axis=1)
        contrib = jnp.einsum(
            "tsb,sab->tsa", dy_picked, weight_now, preferred_element_type=jnp.float32
        )
        onehot = (rows_now[:, None] == row_range[None, :]).astype(jnp.float32)
        added = jnp.einsum("tsa,sr->tra", contrib, onehot, precision=lax.Precision.HIGHEST)
        return (carried + added, None)

    running, _ = lax.scan(advance, running, (rows_part, cols_part, weight_part))
    d_hidden = running.reshape(token_count, ff_dev).astype(jnp.bfloat16)
    grad_scale = 1.0 / math.sqrt(token_count * n_fsdp)
    hidden_blocks = hidden.reshape(token_count, row_count, block_size)
    group_size = math.gcd(slot_total, 48)
    group_count = slot_total // group_size

    def partial_group(packed_item):
        rows_now, cols_now, scale_now = packed_item
        h_picked = jnp.take(hidden_blocks, rows_now, axis=1)
        dy_picked = jnp.take(dy_blocks, cols_now, axis=1)
        product = jnp.einsum(
            "tsa,tsb->sab", h_picked, dy_picked, preferred_element_type=jnp.float32
        )
        return (product * scale_now[:, None, None]).astype(jnp.bfloat16)

    partials = lax.map(
        partial_group,
        (
            row_clip.reshape(group_count, group_size),
            col_index.reshape(group_count, group_size),
            (grad_scale * usable_f).reshape(group_count, group_size),
        ),
    )
    partials = partials.reshape(slot_total, block_size, block_size)
    arrived = lax.all_to_all(partials, "fsdp", split_axis=0, concat_axis=0, tiled=True)
    w_grad = (
        arrived.astype(jnp.float32)
        .reshape(n_fsdp, cap_local, block_size, block_size)
        .sum(axis=0)[None]
    )
    dh_seq = lax.all_to_all(d_hidden, "tensor", split_axis=0, concat_axis=1, tiled=True)
    d_gate, d_up = swiglu_grads(dh_seq, gate_pre, up_pre)
    return (d_gate, d_up, w_grad)


def split_id(slot, cols):
    safe = lax.max(slot, 0)
    if cols & (cols - 1):
        return lax.div(safe, cols), lax.rem(safe, cols)
    return lax.shift_right_logical(safe, cols.bit_length() - 1), lax.bitwise_and(safe, cols - 1)


def sigmoid(value):
    return 0.5 + 0.5 * jnp.tanh(0.5 * value)


def hidden_value(gate_part, up_part):
    gate_f = gate_part.astype(jnp.float32)
    return (gate_f * sigmoid(gate_f) * up_part.astype(jnp.float32)).astype(jnp.bfloat16)


def exchange_kernel(
    scale, ids_ref, ids_vec, gate_hbm, up_hbm, cot_hbm, w_hbm,
    ids_other, con_hbm, wgrad_ref,
    con_ref, ids_in, gate, up, cot, w_all, part, rc, rx0, ry1, ry0, rx1, rz, local, send, recv,
):
    tokens = gate.shape[1]
    cap, block, _ = w_hbm.shape[1:]
    n_z = w_all.shape[3]
    half = block // 2
    cols = cot.shape[0]
    rows = gate.shape[0] // 2
    f = lax.axis_index("fsdp")
    y = lax.axis_index("tensor")
    z, x, k = f // 4, f // 2 % 2, f % 2
    to_core = {"fsdp": f + 1 - 2 * k, "tensor": y}
    to_x = {"fsdp": f + 2 - 4 * x, "tensor": y}
    to_y = {"fsdp": f, "tensor": 1 - y}
    to_z = [{"fsdp": (z + d) % n_z * 4 + x * 2 + k, "tensor": y} for d in range(1, n_z)]
    part_rows = [pl.ds(0, half), pl.ds(half, half)]

    def copy(i, src, dst, to):
        return pltpu.make_async_remote_copy(
            src_ref=src, dst_ref=dst, send_sem=send.at[i], recv_sem=recv.at[i],
            device_id=to, device_id_type=pl.DeviceIdType.MESH,
        )

    def same(i, ref, to):
        return copy(i, ref, ref, to)

    barrier = pltpu.get_barrier_semaphore()
    peers = [to_core, to_x, to_y] + to_z
    for to in peers:
        pl.semaphore_signal(barrier, inc=1, device_id=to, device_id_type=pl.DeviceIdType.MESH)
    own_tokens = pl.ds(pl.multiple_of(y * tokens, tokens), tokens)

    @pl.loop(0, cols, unroll=4)
    def _(i):
        at = pl.ds(pl.multiple_of(i * block, block), block)
        pltpu.make_async_copy(cot_hbm.at[own_tokens, at], cot.at[i], local.at[2]).start()

    @pl.loop(0, 2 * rows, unroll=4)
    def _(i):
        at = pl.ds(pl.multiple_of(i * block, block), block)
        pltpu.make_async_copy(gate_hbm.at[:, at], gate.at[i], local.at[0]).start()
        pltpu.make_async_copy(up_hbm.at[:, at], up.at[i], local.at[1]).start()

    own_w = pltpu.make_async_copy(w_hbm.at[0], w_all.at[k, y, x, z], local.at[3])
    own_w.start()
    pl.semaphore_wait(barrier, len(peers))

    ids_copy = copy(0, ids_vec, ids_in, to_y)
    ids_copy.start()
    ag_x0 = copy(5, w_hbm.at[0, :, part_rows[0]], w_all.at[k, y, x, z, :, part_rows[0]], to_x)
    ag_y1 = copy(6, w_hbm.at[0, :, part_rows[1]], w_all.at[k, y, x, z, :, part_rows[1]], to_y)
    ag_x0.start()
    ag_y1.start()
    ag_z = [copy(1 + d, w_hbm.at[0], w_all.at[k, y, x, z], to_z[d]) for d in range(n_z - 1)]
    for c in ag_z:
        c.start()

    own_w.wait()
    ids_copy.wait_recv()
    ids_local = pltpu.make_async_copy(ids_in, ids_other, local.at[4])
    ids_local.start()
    ids_local.wait()
    ag_x0.wait_recv()
    ag_zx = [same(23 + d, w_all.at[k, y, 1 - x, z, :, part_rows[0]], to_z[d]) for d in range(n_z - 1)]
    ag_y1.wait_recv()
    ag_zy = [
        same(23 + n_z - 1 + d, w_all.at[k, 1 - y, x, z, :, part_rows[1]], to_z[d]) for d in range(n_z - 1)
    ]
    for c in ag_zx + ag_zy:
        c.start()
    for n, ref in enumerate((gate, up, cot)):
        pltpu.make_async_copy(ref, ref, local.at[n]).wait()

    def slots_of(core, xx, ids):
        def visit(step):
            @pl.loop(0, n_z, unroll=2)
            def _(zz):
                first = ((zz * 2 + xx) * 2 + core) * cap
                for q in range(cap):
                    slot = ids[0, first + q]
                    r, c = split_id(slot, cols)
                    step(zz, q, r, c, lax.min(slot + 1, 1).astype(jnp.float32))

        return visit

    def partials(core, t, xx, ids):
        @slots_of(core, xx, ids)
        def _(zz, q, r, c, usable):
            h = hidden_value(gate[r + t * rows], up[r + t * rows])
            got = lax.dot_general(h, cot[c], (((0,), (0,)), ((), ())), preferred_element_type=jnp.float32)
            part[core, t, xx, zz, q] = (got * (usable * scale)).astype(part.dtype)

    con_out = []

    def contribs(core, t, xx, ids):
        @slots_of(core, xx, ids)
        def _(zz, q, r, c, usable):
            got = lax.dot_general(
                cot[c], w_all[core, t, xx, zz, q], (((1,), (1,)), ((), ())), preferred_element_type=jnp.float32
            )
            con_ref[core, t, xx, zz, q] = (got * usable).astype(con_ref.dtype)

        out = pltpu.make_async_copy(con_ref.at[core, t, xx], con_hbm.at[core, t, xx], local.at[5 + len(con_out)])
        out.start()
        con_out.append(out)

    def add(dst, src):
        total = dst[...].astype(jnp.float32) + src[...].astype(jnp.float32)
        dst[...] = total.astype(dst.dtype)

    quads = ((1 - y, 1 - x, ids_other), (y, 1 - x, ids_ref), (1 - y, x, ids_other), (y, x, ids_ref))
    core_p = []

    def send_core(n):
        t, xx, ids = quads[n]
        partials(1 - k, t, xx, ids)
        core_p.append(copy(10 + n, part.at[1 - k, t, xx], rc.at[t, xx], to_core))
        core_p[n].start()

    def add_core(n):
        t, xx, _ = quads[n]
        core_p[n].wait_recv()

        @pl.loop(0, n_z)
        def _(i):
            add(part.at[k, t, xx, i], rc.at[t, xx, i])

    def own_core(n):
        t, xx, ids = quads[n]
        partials(k, t, xx, ids)

    send_core(0)
    own_core(0)
    send_core(1)
    add_core(0)
    far = part.at[k, 1 - y, 1 - x]
    rs_xa = copy(14, far.at[:, :, part_rows[0]], rx0.at[1 - y], to_x)
    rs_ya = copy(15, far.at[:, :, part_rows[1]], ry1.at[1 - x], to_y)
    rs_xa.start()
    rs_ya.start()
    own_core(1)
    send_core(2)
    add_core(1)
    rs_xb = copy(16, part.at[k, y, 1 - x, :, :, part_rows[0]], rx0.at[y], to_x)
    rs_xb.start()
    own_core(2)
    send_core(3)
    add_core(2)
    rs_yb = copy(17, part.at[k, 1 - y, x, :, :, part_rows[1]], ry1.at[x], to_y)
    rs_yb.start()
    own_core(3)

    add_core(3)

    rs_xa.wait_recv()

    @pl.loop(0, n_z)
    def _(i):
        add(part.at[k, 1 - y, x, i, :, part_rows[0]], rx0.at[1 - y, i])

    rs_y0 = copy(18, part.at[k, 1 - y, x, :, :, part_rows[0]], ry0, to_y)
    rs_y0.start()
    rs_ya.wait_recv()

    @pl.loop(0, n_z)
    def _(i):
        add(part.at[k, y, 1 - x, i, :, part_rows[1]], ry1.at[1 - x, i])

    rs_x1 = copy(19, part.at[k, y, 1 - x, :, :, part_rows[1]], rx1, to_x)
    rs_x1.start()

    for c in ag_z:
        c.wait_recv()
    mine = w_all.at[k, y, x]
    ag_ya = same(4, mine.at[:, :, part_rows[0]], to_y)
    ag_xa = same(7, mine.at[:, :, part_rows[1]], to_x)
    ag_ya.start()
    ag_xa.start()
    core_w = [same(29, mine, to_core)]
    core_w[0].start()

    def to_core_w(ref):
        core_w.append(same(29 + len(core_w), ref, to_core))
        core_w[-1].start()

    contribs(k, y, x, ids_ref)
    for c in ag_zx:
        c.wait_recv()
    ag_yb = same(8, w_all.at[k, y, 1 - x, :, :, part_rows[0]], to_y)
    ag_yb.start()
    to_core_w(w_all.at[k, y, 1 - x, :, :, part_rows[0]])
    for c in ag_zy:
        c.wait_recv()
    ag_xb = same(9, w_all.at[k, 1 - y, x, :, :, part_rows[1]], to_x)
    ag_xb.start()
    to_core_w(w_all.at[k, 1 - y, x, :, :, part_rows[1]])

    rs_z = []

    def send_z(p, last, into, came, came_into):
        last.wait_recv()
        came.wait_recv()

        @pl.loop(0, n_z)
        def _(i):
            ref = part.at[k, y, x, i, :, part_rows[p]]
            total = ref[...].astype(jnp.float32) + into[i].astype(jnp.float32)
            ref[...] = (total + came_into[i].astype(jnp.float32)).astype(ref.dtype)

        for d in range(n_z - 1):
            src = part.at[k, y, x, (z + d + 1) % n_z, :, part_rows[p]]
            c = copy(37 + p * (n_z - 1) + d, src, rz.at[d, p], to_z[d])
            c.start()
            rs_z.append(c)

    send_z(0, rs_xb, rx0.at[y], rs_y0, ry0)
    send_z(1, rs_yb, ry1.at[x], rs_x1, rx1)

    core_w[0].wait_recv()
    contribs(1 - k, y, x, ids_ref)
    ag_ya.wait_recv()
    to_core_w(w_all.at[k, 1 - y, x, :, :, part_rows[0]])
    contribs(k, 1 - y, x, ids_other)
    ag_xa.wait_recv()
    to_core_w(w_all.at[k, y, 1 - x, :, :, part_rows[1]])
    contribs(k, y, 1 - x, ids_ref)
    for c in (core_w[2], core_w[3]):
        c.wait_recv()
    contribs(1 - k, 1 - y, x, ids_other)
    for c in (core_w[1], core_w[4]):
        c.wait_recv()
    contribs(1 - k, y, 1 - x, ids_ref)
    ag_yb.wait_recv()
    to_core_w(w_all.at[k, 1 - y, 1 - x, :, :, part_rows[0]])
    ag_xb.wait_recv()
    to_core_w(w_all.at[k, 1 - y, 1 - x, :, :, part_rows[1]])
    contribs(k, 1 - y, 1 - x, ids_other)

    for c in rs_z:
        c.wait_recv()
    for p in range(2):
        total = part[k, y, x, z, :, part_rows[p]].astype(jnp.float32)
        for d in range(n_z - 1):
            total = total + rz[d, p].astype(jnp.float32)
        wgrad_ref[0, :, part_rows[p]] = total
    for c in core_w[5:]:
        c.wait_recv()
    contribs(1 - k, 1 - y, 1 - x, ids_other)
    sent = [ids_copy, ag_x0, ag_y1, ag_xa, ag_ya, ag_xb, ag_yb, rs_xa, rs_ya, rs_xb, rs_yb, rs_x1, rs_y0]
    for c in sent + ag_z + ag_zx + ag_zy + core_p + core_w + rs_z:
        c.wait_send()
    for c in con_out:
        c.wait()


def exchange(gate, up, cot, w, ids, scale):
    tokens, ff = gate.shape
    cap, block = w.shape[1:3]
    bf16 = jnp.bfloat16
    any_spec = pl.BlockSpec(memory_space=pltpu.HBM)
    smem = pl.BlockSpec(memory_space=pltpu.SMEM)
    whole = pl.BlockSpec(memory_space=pltpu.VMEM)
    n_z = lax.axis_size("fsdp") // 4
    half = block // 2
    return pl.pallas_call(
        functools.partial(exchange_kernel, scale),
        out_shape=[
            jax.ShapeDtypeStruct(ids.shape, ids.dtype),
            jax.ShapeDtypeStruct((2, 2, 2, n_z, cap, tokens, block), bf16),
            jax.ShapeDtypeStruct(w.shape, jnp.float32),
        ],
        in_specs=[smem, any_spec, any_spec, any_spec, any_spec, any_spec],
        out_specs=[smem, any_spec, whole],
        scratch_shapes=[
            pltpu.VMEM((2, 2, 2, n_z, cap, tokens, block), bf16),
            pltpu.VMEM(ids.shape, ids.dtype),
            pltpu.VMEM((ff // block, tokens, block), bf16),
            pltpu.VMEM((ff // block, tokens, block), bf16),
            pltpu.VMEM((cot.shape[1] // block, tokens, block), bf16),
            pltpu.VMEM((2, 2, 2, n_z, cap, block, block), bf16),
            pltpu.VMEM((2, 2, 2, n_z, cap, block, block), bf16),
            pltpu.VMEM((2, 2, n_z, cap, block, block), bf16),
            pltpu.VMEM((2, n_z, cap, half, block), bf16),
            pltpu.VMEM((2, n_z, cap, half, block), bf16),
            pltpu.VMEM((n_z, cap, half, block), bf16),
            pltpu.VMEM((n_z, cap, half, block), bf16),
            pltpu.VMEM((n_z - 1, 2, cap, half, block), bf16),
            pltpu.SemaphoreType.DMA((13,)),
            pltpu.SemaphoreType.DMA((37 + 2 * (n_z - 1),)),
            pltpu.SemaphoreType.DMA((37 + 2 * (n_z - 1),)),
        ],
        compiler_params=pltpu.CompilerParams(
            collective_id=0, has_side_effects=True, vmem_limit_bytes=60 * MIB
        ),
    )(ids, ids, gate, up, cot, w)


def grads_kernel(
    cols, ids_ref, other_ref, con_hbm, wgrad_in, gate_ref, up_ref,
    dgate_ref, dup_ref, wgrad_out, dh_ref, con_ref, con_sem, wgrad_sem,
):
    n_z, cap, _, block = con_ref.shape[3:]
    blocks = dh_ref.shape[0]
    per = gate_ref.shape[1] // block
    y = lax.axis_index("tensor")
    step = pl.program_id(0)

    @pl.when(step == 0)
    def _():
        con_copy = pltpu.make_async_copy(con_hbm, con_ref, con_sem)
        con_copy.start()
        pltpu.make_async_copy(wgrad_in, wgrad_out, wgrad_sem).start()
        dh_ref[...] = jnp.zeros_like(dh_ref)
        con_copy.wait()
        for t, ids in ((y, ids_ref), (1 - y, other_ref)):
            for s in range(4 * n_z * cap):
                f = s // cap
                r = split_id(ids[0, s], cols)[0] + t * (blocks // 2)
                dh_ref[r] += con_ref[f % 2, t, f // 2 % 2, f // 4, s % cap].astype(jnp.float32)

    for j in range(per):
        at = slice(j * block, (j + 1) * block)
        gate_f = gate_ref[:, at].astype(jnp.float32)
        dh = dh_ref[step * per + j]
        sig = sigmoid(gate_f)
        silu = gate_f * sig
        dup_ref[:, at] = (dh * silu).astype(dup_ref.dtype)
        slope = sig + silu * (1.0 - sig)
        dgate_ref[:, at] = (dh * up_ref[:, at].astype(jnp.float32) * slope).astype(dgate_ref.dtype)

    @pl.when(step == pl.num_programs(0) - 1)
    def _():
        pltpu.make_async_copy(wgrad_in, wgrad_out, wgrad_sem).wait()


def local_grads(ids, other, contrib, w_grad, cols, gate, up):
    tokens, ff = gate.shape
    steps = 8
    width = ff // steps
    block = contrib.shape[-1]
    smem = pl.BlockSpec(memory_space=pltpu.SMEM)
    hbm = pl.BlockSpec(memory_space=pltpu.HBM)
    tile = pl.BlockSpec((tokens, width), lambda i: (0, i))
    return pl.pallas_call(
        functools.partial(grads_kernel, cols),
        grid=(steps,),
        out_shape=[jax.ShapeDtypeStruct(gate.shape, jnp.bfloat16)] * 2
        + [jax.ShapeDtypeStruct(w_grad.shape, w_grad.dtype)],
        in_specs=[smem, smem, hbm, hbm, tile, tile],
        out_specs=[tile, tile, hbm],
        scratch_shapes=[
            pltpu.VMEM((ff // block, tokens, block), jnp.float32),
            pltpu.VMEM(contrib.shape, contrib.dtype),
            pltpu.SemaphoreType.DMA,
            pltpu.SemaphoreType.DMA,
        ],
        compiler_params=pltpu.CompilerParams(vmem_limit_bytes=60 * MIB),
    )(ids, other, contrib, w_grad, gate, up)


def body(gate_pre, up_pre, cotangent, w_slots, slot_ids):
    scale = 1.0 / math.sqrt(cotangent.shape[0] * lax.axis_size("fsdp"))
    other, contrib, w_grad = exchange(gate_pre, up_pre, cotangent, w_slots, slot_ids, scale)
    cols = cotangent.shape[1] // w_slots.shape[2]
    return tuple(local_grads(slot_ids, other, contrib, w_grad, cols, gate_pre, up_pre))


def solution(mesh):
    placed = (
        P(("fsdp", "tensor"), None),
        P(("fsdp", "tensor"), None),
        P("fsdp", None),
        P("tensor", "fsdp", None, None),
        P("tensor", None),
    )
    small = mesh.shape["tensor"] == 2 and mesh.shape["fsdp"] == 16
    return jax.shard_map(
        body if small else wide_body,
        mesh=mesh,
        in_specs=placed,
        out_specs=(
            P(("fsdp", "tensor"), None),
            P(("fsdp", "tensor"), None),
            P("tensor", "fsdp", None, None),
        ),
        check_vma=False,
    )
```

```python
import functools
import math

import jax
import jax.numpy as jnp
from jax import lax
from jax.experimental import pallas as pl
from jax.experimental.pallas import tpu as pltpu
from jax.sharding import PartitionSpec as P

MIB = 1 << 20


def swiglu_value(gate_part, up_part):
    gate_f = gate_part.astype(jnp.float32)
    gate_sig = jax.nn.sigmoid(gate_f)
    return (gate_f * gate_sig * up_part.astype(jnp.float32)).astype(jnp.bfloat16)


def swiglu_grads(dh_part, gate_part, up_part):
    gate_f = gate_part.astype(jnp.float32)
    up_f = up_part.astype(jnp.float32)
    gate_sig = jax.nn.sigmoid(gate_f)
    dh_f = dh_part.astype(jnp.float32)
    grad_gate = (dh_f * up_f * (gate_sig * (1.0 + gate_f * (1.0 - gate_sig)))).astype(jnp.bfloat16)
    grad_up = (dh_f * (gate_f * gate_sig)).astype(jnp.bfloat16)
    return (grad_gate, grad_up)


def wide_body(gate_pre, up_pre, cotangent, w_slots, slot_ids):
    n_fsdp = lax.axis_size("fsdp")
    block_size = w_slots.shape[2]
    token_count = cotangent.shape[0]
    model_width = cotangent.shape[1]
    col_count = model_width // block_size
    ff_dev = gate_pre.shape[1] // lax.axis_size("tensor")
    row_count = ff_dev // block_size
    slot_total = slot_ids.shape[1]
    cap_local = w_slots.shape[1]
    slot_list = slot_ids[0]
    usable = slot_list >= 0
    safe_ids = jnp.maximum(slot_list, 0)
    row_index = jnp.where(usable, safe_ids // col_count, row_count)
    col_index = safe_ids % col_count
    row_clip = jnp.minimum(row_index, row_count - 1)
    usable_f = usable.astype(jnp.float32)
    row_range = jnp.arange(row_count, dtype=jnp.int32)
    dy_blocks = cotangent.reshape(token_count, col_count, block_size)
    hidden_seq = swiglu_value(gate_pre, up_pre)
    hidden = lax.all_to_all(hidden_seq, "tensor", split_axis=1, concat_axis=0, tiled=True)
    start_sum = jnp.zeros((token_count, row_count, block_size), jnp.float32)
    running = start_sum
    shard_piece = lax.all_gather(w_slots, "fsdp", axis=1, tiled=True)
    slot_count = shard_piece.shape[1]
    sub_size = math.gcd(slot_count, 48)
    rows_part = row_index.reshape(slot_count // sub_size, sub_size)
    cols_part = col_index.reshape(slot_count // sub_size, sub_size)
    weight_part = shard_piece[0].reshape(slot_count // sub_size, sub_size, block_size, block_size)

    def advance(carried, packed_item):
        rows_now, cols_now, weight_now = packed_item
        dy_picked = jnp.take(dy_blocks, cols_now, axis=1)
        contrib = jnp.einsum(
            "tsb,sab->tsa", dy_picked, weight_now, preferred_element_type=jnp.float32
        )
        onehot = (rows_now[:, None] == row_range[None, :]).astype(jnp.float32)
        added = jnp.einsum("tsa,sr->tra", contrib, onehot, precision=lax.Precision.HIGHEST)
        return (carried + added, None)

    running, _ = lax.scan(advance, running, (rows_part, cols_part, weight_part))
    d_hidden = running.reshape(token_count, ff_dev).astype(jnp.bfloat16)
    grad_scale = 1.0 / math.sqrt(token_count * n_fsdp)
    hidden_blocks = hidden.reshape(token_count, row_count, block_size)
    group_size = math.gcd(slot_total, 48)
    group_count = slot_total // group_size

    def partial_group(packed_item):
        rows_now, cols_now, scale_now = packed_item
        h_picked = jnp.take(hidden_blocks, rows_now, axis=1)
        dy_picked = jnp.take(dy_blocks, cols_now, axis=1)
        product = jnp.einsum(
            "tsa,tsb->sab", h_picked, dy_picked, preferred_element_type=jnp.float32
        )
        return (product * scale_now[:, None, None]).astype(jnp.bfloat16)

    partials = lax.map(
        partial_group,
        (
            row_clip.reshape(group_count, group_size),
            col_index.reshape(group_count, group_size),
            (grad_scale * usable_f).reshape(group_count, group_size),
        ),
    )
    partials = partials.reshape(slot_total, block_size, block_size)
    arrived = lax.all_to_all(partials, "fsdp", split_axis=0, concat_axis=0, tiled=True)
    w_grad = (
        arrived.astype(jnp.float32)
        .reshape(n_fsdp, cap_local, block_size, block_size)
        .sum(axis=0)[None]
    )
    dh_seq = lax.all_to_all(d_hidden, "tensor", split_axis=0, concat_axis=1, tiled=True)
    d_gate, d_up = swiglu_grads(dh_seq, gate_pre, up_pre)
    return (d_gate, d_up, w_grad)


def split_id(slot, cols):
    safe = lax.max(slot, 0)
    if cols & (cols - 1):
        return lax.div(safe, cols), lax.rem(safe, cols)
    return lax.shift_right_logical(safe, cols.bit_length() - 1), lax.bitwise_and(safe, cols - 1)


def sigmoid(value):
    return 0.5 + 0.5 * jnp.tanh(0.5 * value)


def hidden_value(gate_part, up_part):
    gate_f = gate_part.astype(jnp.float32)
    return (gate_f * sigmoid(gate_f) * up_part.astype(jnp.float32)).astype(jnp.bfloat16)


def exchange_kernel(
    scale, ids_ref, ids_vec, gate_hbm, up_hbm, cot_hbm, w_hbm,
    ids_other, con_hbm, wgrad_ref,
    con_ref, ids_in, gate, up, cot, w_all, part, rc, rx0, ry1, ry0, rx1, rz, local, send, recv,
):
    tokens = gate.shape[1]
    cap, block, _ = w_hbm.shape[1:]
    n_z = w_all.shape[3]
    half = block // 2
    cols = cot.shape[0]
    rows = gate.shape[0] // 2
    f = lax.axis_index("fsdp")
    y = lax.axis_index("tensor")
    z, x, k = f // 4, f // 2 % 2, f % 2
    to_core = {"fsdp": f + 1 - 2 * k, "tensor": y}
    to_x = {"fsdp": f + 2 - 4 * x, "tensor": y}
    to_y = {"fsdp": f, "tensor": 1 - y}
    to_z = [{"fsdp": (z + d) % n_z * 4 + x * 2 + k, "tensor": y} for d in range(1, n_z)]
    part_rows = [pl.ds(0, half), pl.ds(half, half)]

    def copy(i, src, dst, to):
        return pltpu.make_async_remote_copy(
            src_ref=src, dst_ref=dst, send_sem=send.at[i], recv_sem=recv.at[i],
            device_id=to, device_id_type=pl.DeviceIdType.MESH,
        )

    def same(i, ref, to):
        return copy(i, ref, ref, to)

    barrier = pltpu.get_barrier_semaphore()
    peers = [to_core, to_x, to_y] + to_z
    for to in peers:
        pl.semaphore_signal(barrier, inc=1, device_id=to, device_id_type=pl.DeviceIdType.MESH)
    own_tokens = pl.ds(pl.multiple_of(y * tokens, tokens), tokens)

    @pl.loop(0, cols, unroll=4)
    def _(i):
        at = pl.ds(pl.multiple_of(i * block, block), block)
        pltpu.make_async_copy(cot_hbm.at[own_tokens, at], cot.at[i], local.at[2]).start()

    @pl.loop(0, 2 * rows, unroll=4)
    def _(i):
        at = pl.ds(pl.multiple_of(i * block, block), block)
        pltpu.make_async_copy(gate_hbm.at[:, at], gate.at[i], local.at[0]).start()
        pltpu.make_async_copy(up_hbm.at[:, at], up.at[i], local.at[1]).start()

    own_w = pltpu.make_async_copy(w_hbm.at[0], w_all.at[k, y, x, z], local.at[3])
    own_w.start()
    pl.semaphore_wait(barrier, len(peers))

    ids_copy = copy(0, ids_vec, ids_in, to_y)
    ids_copy.start()
    ag_x0 = copy(5, w_hbm.at[0], w_all.at[k, y, x, z], to_x)
    ag_y1 = copy(6, w_hbm.at[0], w_all.at[k, y, x, z], to_y)
    ag_x0.start()
    ag_y1.start()
    ag_z = [copy(1 + d, w_hbm.at[0], w_all.at[k, y, x, z], to_z[d]) for d in range(n_z - 1)]
    for c in ag_z:
        c.start()

    own_w.wait()
    ids_copy.wait_recv()
    ids_local = pltpu.make_async_copy(ids_in, ids_other, local.at[4])
    ids_local.start()
    ids_local.wait()
    for n, ref in enumerate((gate, up, cot)):
        pltpu.make_async_copy(ref, ref, local.at[n]).wait()

    def slots_of(core, xx, ids):
        def visit(step):
            @pl.loop(0, n_z, unroll=2)
            def _(zz):
                first = ((zz * 2 + xx) * 2 + core) * cap
                for q in range(cap):
                    slot = ids[0, first + q]
                    r, c = split_id(slot, cols)
                    step(zz, q, r, c, lax.min(slot + 1, 1).astype(jnp.float32))

        return visit

    def partials(core, t, xx, ids):
        @slots_of(core, xx, ids)
        def _(zz, q, r, c, usable):
            h = hidden_value(gate[r + t * rows], up[r + t * rows])
            got = lax.dot_general(h, cot[c], (((0,), (0,)), ((), ())), preferred_element_type=jnp.float32)
            part[core, t, xx, zz, q] = (got * (usable * scale)).astype(part.dtype)

    con_out = []

    def contribs(core, t, xx, ids):
        @slots_of(core, xx, ids)
        def _(zz, q, r, c, usable):
            got = lax.dot_general(
                cot[c], w_all[core, t, xx, zz, q], (((1,), (1,)), ((), ())), preferred_element_type=jnp.float32
            )
            con_ref[core, t, xx, zz, q] = (got * usable).astype(con_ref.dtype)

        out = pltpu.make_async_copy(con_ref.at[core, t, xx], con_hbm.at[core, t, xx], local.at[5 + len(con_out)])
        out.start()
        con_out.append(out)

    def add(dst, src):
        total = dst[...].astype(jnp.float32) + src[...].astype(jnp.float32)
        dst[...] = total.astype(dst.dtype)

    quads = ((1 - y, 1 - x, ids_other), (y, 1 - x, ids_ref), (1 - y, x, ids_other), (y, x, ids_ref))
    core_p = []

    def send_core(n):
        t, xx, ids = quads[n]
        partials(1 - k, t, xx, ids)
        core_p.append(copy(10 + n, part.at[1 - k, t, xx], rc.at[t, xx], to_core))
        core_p[n].start()

    def add_core(n):
        t, xx, _ = quads[n]
        core_p[n].wait_recv()

        @pl.loop(0, n_z)
        def _(i):
            add(part.at[k, t, xx, i], rc.at[t, xx, i])

    def own_core(n):
        t, xx, ids = quads[n]
        partials(k, t, xx, ids)

    send_core(0)
    ag_x0.wait_recv()
    ag_zx = [same(23 + d, w_all.at[k, y, 1 - x, z, :, part_rows[0]], to_z[d]) for d in range(n_z - 1)]
    ag_y1.wait_recv()
    ag_zy = [
        same(23 + n_z - 1 + d, w_all.at[k, 1 - y, x, z, :, part_rows[1]], to_z[d]) for d in range(n_z - 1)
    ]
    for c in ag_zx + ag_zy:
        c.start()
    own_core(0)
    add_core(0)
    far = part.at[k, 1 - y, 1 - x]
    rs_xa = copy(14, far.at[:, :, part_rows[0]], rx0.at[1 - y], to_x)
    rs_ya = copy(15, far.at[:, :, part_rows[1]], ry1.at[1 - x], to_y)
    rs_xa.start()
    rs_ya.start()
    send_core(1)
    own_core(1)
    send_core(2)
    add_core(1)
    rs_xb = copy(16, part.at[k, y, 1 - x, :, :, part_rows[0]], rx0.at[y], to_x)
    rs_xb.start()
    own_core(2)
    send_core(3)
    add_core(2)
    rs_yb = copy(17, part.at[k, 1 - y, x, :, :, part_rows[1]], ry1.at[x], to_y)
    rs_yb.start()
    own_core(3)

    add_core(3)

    rs_xa.wait_recv()

    @pl.loop(0, n_z)
    def _(i):
        add(part.at[k, 1 - y, x, i, :, part_rows[0]], rx0.at[1 - y, i])

    rs_y0 = copy(18, part.at[k, 1 - y, x, :, :, part_rows[0]], ry0, to_y)
    rs_y0.start()
    rs_ya.wait_recv()

    @pl.loop(0, n_z)
    def _(i):
        add(part.at[k, y, 1 - x, i, :, part_rows[1]], ry1.at[1 - x, i])

    rs_x1 = copy(19, part.at[k, y, 1 - x, :, :, part_rows[1]], rx1, to_x)
    rs_x1.start()

    for c in ag_z:
        c.wait_recv()
    mine = w_all.at[k, y, x]
    ag_ya, ag_xa = [], []
    for d in range(n_z - 1):
        came = mine.at[(z + d + 1) % n_z]
        ag_ya.append(same(37 + 2 * (n_z - 1) + d, came.at[:, part_rows[0]], to_y))
        ag_xa.append(same(37 + 3 * (n_z - 1) + d, came.at[:, part_rows[1]], to_x))
        ag_ya[d].start()
        ag_xa[d].start()
    core_w = [same(29, mine, to_core)]
    core_w[0].start()

    def to_core_w(ref):
        core_w.append(same(29 + len(core_w), ref, to_core))
        core_w[-1].start()

    contribs(k, y, x, ids_ref)
    for c in ag_zx:
        c.wait_recv()
    ag_yb = same(8, w_all.at[k, y, 1 - x, :, :, part_rows[0]], to_y)
    ag_yb.start()
    to_core_w(w_all.at[k, y, 1 - x, :, :, part_rows[0]])
    for c in ag_zy:
        c.wait_recv()
    ag_xb = same(9, w_all.at[k, 1 - y, x, :, :, part_rows[1]], to_x)
    ag_xb.start()
    to_core_w(w_all.at[k, 1 - y, x, :, :, part_rows[1]])

    rs_z = []

    def send_z(p, last, into, came, came_into):
        last.wait_recv()
        came.wait_recv()

        @pl.loop(0, n_z)
        def _(i):
            ref = part.at[k, y, x, i, :, part_rows[p]]
            total = ref[...].astype(jnp.float32) + into[i].astype(jnp.float32)
            ref[...] = (total + came_into[i].astype(jnp.float32)).astype(ref.dtype)

        for d in range(n_z - 1):
            src = part.at[k, y, x, (z + d + 1) % n_z, :, part_rows[p]]
            c = copy(37 + p * (n_z - 1) + d, src, rz.at[d, p], to_z[d])
            c.start()
            rs_z.append(c)

    send_z(0, rs_xb, rx0.at[y], rs_y0, ry0)
    send_z(1, rs_yb, ry1.at[x], rs_x1, rx1)

    core_w[0].wait_recv()
    contribs(1 - k, y, x, ids_ref)
    for c in ag_ya:
        c.wait_recv()
    to_core_w(w_all.at[k, 1 - y, x, :, :, part_rows[0]])
    contribs(k, 1 - y, x, ids_other)
    for c in ag_xa:
        c.wait_recv()
    to_core_w(w_all.at[k, y, 1 - x, :, :, part_rows[1]])
    contribs(k, y, 1 - x, ids_ref)
    for c in (core_w[2], core_w[3]):
        c.wait_recv()
    contribs(1 - k, 1 - y, x, ids_other)
    for c in (core_w[1], core_w[4]):
        c.wait_recv()
    contribs(1 - k, y, 1 - x, ids_ref)
    ag_yb.wait_recv()
    to_core_w(w_all.at[k, 1 - y, 1 - x, :, :, part_rows[0]])
    ag_xb.wait_recv()
    to_core_w(w_all.at[k, 1 - y, 1 - x, :, :, part_rows[1]])
    contribs(k, 1 - y, 1 - x, ids_other)

    for c in rs_z:
        c.wait_recv()
    for p in range(2):
        total = part[k, y, x, z, :, part_rows[p]].astype(jnp.float32)
        for d in range(n_z - 1):
            total = total + rz[d, p].astype(jnp.float32)
        wgrad_ref[0, :, part_rows[p]] = total
    for c in core_w[5:]:
        c.wait_recv()
    contribs(1 - k, 1 - y, 1 - x, ids_other)
    sent = [ids_copy, ag_x0, ag_y1, ag_xb, ag_yb, rs_xa, rs_ya, rs_xb, rs_yb, rs_x1, rs_y0]
    for c in sent + ag_z + ag_xa + ag_ya + ag_zx + ag_zy + core_p + core_w + rs_z:
        c.wait_send()
    for c in con_out:
        c.wait()


def exchange(gate, up, cot, w, ids, scale):
    tokens, ff = gate.shape
    cap, block = w.shape[1:3]
    bf16 = jnp.bfloat16
    any_spec = pl.BlockSpec(memory_space=pltpu.HBM)
    smem = pl.BlockSpec(memory_space=pltpu.SMEM)
    whole = pl.BlockSpec(memory_space=pltpu.VMEM)
    n_z = lax.axis_size("fsdp") // 4
    half = block // 2
    return pl.pallas_call(
        functools.partial(exchange_kernel, scale),
        out_shape=[
            jax.ShapeDtypeStruct(ids.shape, ids.dtype),
            jax.ShapeDtypeStruct((2, 2, 2, n_z, cap, tokens, block), bf16),
            jax.ShapeDtypeStruct(w.shape, jnp.float32),
        ],
        in_specs=[smem, any_spec, any_spec, any_spec, any_spec, any_spec],
        out_specs=[smem, any_spec, whole],
        scratch_shapes=[
            pltpu.VMEM((2, 2, 2, n_z, cap, tokens, block), bf16),
            pltpu.VMEM(ids.shape, ids.dtype),
            pltpu.VMEM((ff // block, tokens, block), bf16),
            pltpu.VMEM((ff // block, tokens, block), bf16),
            pltpu.VMEM((cot.shape[1] // block, tokens, block), bf16),
            pltpu.VMEM((2, 2, 2, n_z, cap, block, block), bf16),
            pltpu.VMEM((2, 2, 2, n_z, cap, block, block), bf16),
            pltpu.VMEM((2, 2, n_z, cap, block, block), bf16),
            pltpu.VMEM((2, n_z, cap, half, block), bf16),
            pltpu.VMEM((2, n_z, cap, half, block), bf16),
            pltpu.VMEM((n_z, cap, half, block), bf16),
            pltpu.VMEM((n_z, cap, half, block), bf16),
            pltpu.VMEM((n_z - 1, 2, cap, half, block), bf16),
            pltpu.SemaphoreType.DMA((13,)),
            pltpu.SemaphoreType.DMA((37 + 4 * (n_z - 1),)),
            pltpu.SemaphoreType.DMA((37 + 4 * (n_z - 1),)),
        ],
        compiler_params=pltpu.CompilerParams(
            collective_id=0, has_side_effects=True, vmem_limit_bytes=60 * MIB
        ),
    )(ids, ids, gate, up, cot, w)


def grads_kernel(
    cols, ids_ref, other_ref, con_hbm, wgrad_in, gate_ref, up_ref,
    dgate_ref, dup_ref, wgrad_out, dh_own, dh_other, con_ref, con_sem, wgrad_sem,
):
    n_z, cap, _, block = con_ref.shape[3:]
    per = gate_ref.shape[1] // block
    y = lax.axis_index("tensor")
    step = pl.program_id(0)

    @pl.when(step == 0)
    def _():
        con_copy = pltpu.make_async_copy(con_hbm, con_ref, con_sem)
        con_copy.start()
        pltpu.make_async_copy(wgrad_in, wgrad_out, wgrad_sem).start()
        dh_own[...] = jnp.zeros_like(dh_own)
        dh_other[...] = jnp.zeros_like(dh_other)
        con_copy.wait()
        for s in range(4 * n_z * cap):
            f = s // cap
            for t, ids, dh_ref in ((y, ids_ref, dh_own), (1 - y, other_ref, dh_other)):
                r = split_id(ids[0, s], cols)[0]
                dh_ref[r] += con_ref[f % 2, t, f // 2 % 2, f // 4, s % cap].astype(jnp.float32)

    def apply(first, dh_ref):
        for j in range(per):
            at = slice(j * block, (j + 1) * block)
            gate_f = gate_ref[:, at].astype(jnp.float32)
            dh = dh_ref[first + j]
            sig = sigmoid(gate_f)
            silu = gate_f * sig
            dup_ref[:, at] = (dh * silu).astype(dup_ref.dtype)
            slope = sig + silu * (1.0 - sig)
            dgate_ref[:, at] = (dh * up_ref[:, at].astype(jnp.float32) * slope).astype(dgate_ref.dtype)

    half_steps = pl.num_programs(0) // 2
    first = step % half_steps * per

    @pl.when(step // half_steps == y)
    def _():
        apply(first, dh_own)

    @pl.when(step // half_steps != y)
    def _():
        apply(first, dh_other)

    @pl.when(step == pl.num_programs(0) - 1)
    def _():
        pltpu.make_async_copy(wgrad_in, wgrad_out, wgrad_sem).wait()


def local_grads(ids, other, contrib, w_grad, cols, gate, up):
    tokens, ff = gate.shape
    steps = 8
    width = ff // steps
    block = contrib.shape[-1]
    smem = pl.BlockSpec(memory_space=pltpu.SMEM)
    hbm = pl.BlockSpec(memory_space=pltpu.HBM)
    tile = pl.BlockSpec((tokens, width), lambda i: (0, i))
    return pl.pallas_call(
        functools.partial(grads_kernel, cols),
        grid=(steps,),
        out_shape=[jax.ShapeDtypeStruct(gate.shape, jnp.bfloat16)] * 2
        + [jax.ShapeDtypeStruct(w_grad.shape, w_grad.dtype)],
        in_specs=[smem, smem, hbm, hbm, tile, tile],
        out_specs=[tile, tile, hbm],
        scratch_shapes=[
            pltpu.VMEM((ff // block // 2, tokens, block), jnp.float32),
            pltpu.VMEM((ff // block // 2, tokens, block), jnp.float32),
            pltpu.VMEM(contrib.shape, contrib.dtype),
            pltpu.SemaphoreType.DMA,
            pltpu.SemaphoreType.DMA,
        ],
        compiler_params=pltpu.CompilerParams(vmem_limit_bytes=60 * MIB),
    )(ids, other, contrib, w_grad, gate, up)


def body(gate_pre, up_pre, cotangent, w_slots, slot_ids):
    scale = 1.0 / math.sqrt(cotangent.shape[0] * lax.axis_size("fsdp"))
    other, contrib, w_grad = exchange(gate_pre, up_pre, cotangent, w_slots, slot_ids, scale)
    cols = cotangent.shape[1] // w_slots.shape[2]
    return tuple(local_grads(slot_ids, other, contrib, w_grad, cols, gate_pre, up_pre))


def solution(mesh):
    placed = (
        P(("fsdp", "tensor"), None),
        P(("fsdp", "tensor"), None),
        P("fsdp", None),
        P("tensor", "fsdp", None, None),
        P("tensor", None),
    )
    small = mesh.shape["tensor"] == 2 and mesh.shape["fsdp"] == 16
    return jax.shard_map(
        body if small else wide_body,
        mesh=mesh,
        in_specs=placed,
        out_specs=(
            P(("fsdp", "tensor"), None),
            P(("fsdp", "tensor"), None),
            P("tensor", "fsdp", None, None),
        ),
        check_vma=False,
    )
```

```python
import functools
import math

import jax
import jax.numpy as jnp
from jax import lax
from jax.experimental import pallas as pl
from jax.experimental.pallas import tpu as pltpu
from jax.sharding import PartitionSpec as P

MIB = 1 << 20


def swiglu_value(gate_part, up_part):
    gate_f = gate_part.astype(jnp.float32)
    gate_sig = jax.nn.sigmoid(gate_f)
    return (gate_f * gate_sig * up_part.astype(jnp.float32)).astype(jnp.bfloat16)


def swiglu_grads(dh_part, gate_part, up_part):
    gate_f = gate_part.astype(jnp.float32)
    up_f = up_part.astype(jnp.float32)
    gate_sig = jax.nn.sigmoid(gate_f)
    dh_f = dh_part.astype(jnp.float32)
    grad_gate = (dh_f * up_f * (gate_sig * (1.0 + gate_f * (1.0 - gate_sig)))).astype(jnp.bfloat16)
    grad_up = (dh_f * (gate_f * gate_sig)).astype(jnp.bfloat16)
    return (grad_gate, grad_up)


def wide_body(gate_pre, up_pre, cotangent, w_slots, slot_ids):
    n_fsdp = lax.axis_size("fsdp")
    block_size = w_slots.shape[2]
    token_count = cotangent.shape[0]
    model_width = cotangent.shape[1]
    col_count = model_width // block_size
    ff_dev = gate_pre.shape[1] // lax.axis_size("tensor")
    row_count = ff_dev // block_size
    slot_total = slot_ids.shape[1]
    cap_local = w_slots.shape[1]
    slot_list = slot_ids[0]
    usable = slot_list >= 0
    safe_ids = jnp.maximum(slot_list, 0)
    row_index = jnp.where(usable, safe_ids // col_count, row_count)
    col_index = safe_ids % col_count
    row_clip = jnp.minimum(row_index, row_count - 1)
    usable_f = usable.astype(jnp.float32)
    row_range = jnp.arange(row_count, dtype=jnp.int32)
    dy_blocks = cotangent.reshape(token_count, col_count, block_size)
    hidden_seq = swiglu_value(gate_pre, up_pre)
    hidden = lax.all_to_all(hidden_seq, "tensor", split_axis=1, concat_axis=0, tiled=True)
    start_sum = jnp.zeros((token_count, row_count, block_size), jnp.float32)
    running = start_sum
    shard_piece = lax.all_gather(w_slots, "fsdp", axis=1, tiled=True)
    slot_count = shard_piece.shape[1]
    sub_size = math.gcd(slot_count, 48)
    rows_part = row_index.reshape(slot_count // sub_size, sub_size)
    cols_part = col_index.reshape(slot_count // sub_size, sub_size)
    weight_part = shard_piece[0].reshape(slot_count // sub_size, sub_size, block_size, block_size)

    def advance(carried, packed_item):
        rows_now, cols_now, weight_now = packed_item
        dy_picked = jnp.take(dy_blocks, cols_now, axis=1)
        contrib = jnp.einsum(
            "tsb,sab->tsa", dy_picked, weight_now, preferred_element_type=jnp.float32
        )
        onehot = (rows_now[:, None] == row_range[None, :]).astype(jnp.float32)
        added = jnp.einsum("tsa,sr->tra", contrib, onehot, precision=lax.Precision.HIGHEST)
        return (carried + added, None)

    running, _ = lax.scan(advance, running, (rows_part, cols_part, weight_part))
    d_hidden = running.reshape(token_count, ff_dev).astype(jnp.bfloat16)
    grad_scale = 1.0 / math.sqrt(token_count * n_fsdp)
    hidden_blocks = hidden.reshape(token_count, row_count, block_size)
    group_size = math.gcd(slot_total, 48)
    group_count = slot_total // group_size

    def partial_group(packed_item):
        rows_now, cols_now, scale_now = packed_item
        h_picked = jnp.take(hidden_blocks, rows_now, axis=1)
        dy_picked = jnp.take(dy_blocks, cols_now, axis=1)
        product = jnp.einsum(
            "tsa,tsb->sab", h_picked, dy_picked, preferred_element_type=jnp.float32
        )
        return (product * scale_now[:, None, None]).astype(jnp.bfloat16)

    partials = lax.map(
        partial_group,
        (
            row_clip.reshape(group_count, group_size),
            col_index.reshape(group_count, group_size),
            (grad_scale * usable_f).reshape(group_count, group_size),
        ),
    )
    partials = partials.reshape(slot_total, block_size, block_size)
    arrived = lax.all_to_all(partials, "fsdp", split_axis=0, concat_axis=0, tiled=True)
    w_grad = (
        arrived.astype(jnp.float32)
        .reshape(n_fsdp, cap_local, block_size, block_size)
        .sum(axis=0)[None]
    )
    dh_seq = lax.all_to_all(d_hidden, "tensor", split_axis=0, concat_axis=1, tiled=True)
    d_gate, d_up = swiglu_grads(dh_seq, gate_pre, up_pre)
    return (d_gate, d_up, w_grad)


def split_id(slot, cols):
    safe = lax.max(slot, 0)
    if cols & (cols - 1):
        return lax.div(safe, cols), lax.rem(safe, cols)
    return lax.shift_right_logical(safe, cols.bit_length() - 1), lax.bitwise_and(safe, cols - 1)


def sigmoid(value):
    return 0.5 + 0.5 * jnp.tanh(0.5 * value)


def hidden_value(gate_part, up_part):
    gate_f = gate_part.astype(jnp.float32)
    return (gate_f * sigmoid(gate_f) * up_part.astype(jnp.float32)).astype(jnp.bfloat16)


def exchange_kernel(
    scale, ids_ref, ids_vec, gate_hbm, up_hbm, cot_hbm, w_hbm,
    ids_other, con_hbm, wgrad_ref,
    con_ref, ids_in, gate, up, cot, w_all, part, rc, rx0, ry1, ry0, rx1, rz, local, send, recv,
):
    tokens = gate.shape[1]
    cap, block, _ = w_hbm.shape[1:]
    n_z = w_all.shape[3]
    half = block // 2
    cols = cot.shape[0]
    rows = gate.shape[0] // 2
    f = lax.axis_index("fsdp")
    y = lax.axis_index("tensor")
    z, x, k = f // 4, f // 2 % 2, f % 2
    to_core = {"fsdp": f + 1 - 2 * k, "tensor": y}
    to_x = {"fsdp": f + 2 - 4 * x, "tensor": y}
    to_y = {"fsdp": f, "tensor": 1 - y}
    to_z = [{"fsdp": (z + d) % n_z * 4 + x * 2 + k, "tensor": y} for d in range(1, n_z)]
    part_rows = [pl.ds(0, half), pl.ds(half, half)]

    def copy(i, src, dst, to):
        return pltpu.make_async_remote_copy(
            src_ref=src, dst_ref=dst, send_sem=send.at[i], recv_sem=recv.at[i],
            device_id=to, device_id_type=pl.DeviceIdType.MESH,
        )

    def same(i, ref, to):
        return copy(i, ref, ref, to)

    barrier = pltpu.get_barrier_semaphore()
    peers = [to_core, to_x, to_y] + to_z
    for to in peers:
        pl.semaphore_signal(barrier, inc=1, device_id=to, device_id_type=pl.DeviceIdType.MESH)
    own_tokens = pl.ds(pl.multiple_of(y * tokens, tokens), tokens)

    @pl.loop(0, cols, unroll=4)
    def _(i):
        at = pl.ds(pl.multiple_of(i * block, block), block)
        pltpu.make_async_copy(cot_hbm.at[own_tokens, at], cot.at[i], local.at[2]).start()

    @pl.loop(0, 2 * rows, unroll=4)
    def _(i):
        at = pl.ds(pl.multiple_of(i * block, block), block)
        pltpu.make_async_copy(gate_hbm.at[:, at], gate.at[i], local.at[0]).start()
        pltpu.make_async_copy(up_hbm.at[:, at], up.at[i], local.at[1]).start()

    own_w = pltpu.make_async_copy(w_hbm.at[0], w_all.at[k, y, x, z], local.at[3])
    own_w.start()
    pl.semaphore_wait(barrier, len(peers))

    ids_copy = copy(0, ids_vec, ids_in, to_y)
    ids_copy.start()
    ag_x0 = copy(5, w_hbm.at[0], w_all.at[k, y, x, z], to_x)
    ag_y1 = copy(6, w_hbm.at[0], w_all.at[k, y, x, z], to_y)
    ag_x0.start()
    ag_y1.start()
    ag_z = [copy(1 + d, w_hbm.at[0], w_all.at[k, y, x, z], to_z[d]) for d in range(n_z - 1)]
    for c in ag_z:
        c.start()

    own_w.wait()
    ids_copy.wait_recv()
    ids_local = pltpu.make_async_copy(ids_in, ids_other, local.at[4])
    ids_local.start()
    ids_local.wait()
    for n, ref in enumerate((gate, up, cot)):
        pltpu.make_async_copy(ref, ref, local.at[n]).wait()

    def slots_of(core, xx, ids):
        def visit(step):
            @pl.loop(0, n_z, unroll=2)
            def _(zz):
                first = ((zz * 2 + xx) * 2 + core) * cap
                for q in range(cap):
                    slot = ids[0, first + q]
                    r, c = split_id(slot, cols)
                    step(zz, q, r, c, lax.min(slot + 1, 1).astype(jnp.float32))

        return visit

    def partials(core, t, xx, ids):
        @slots_of(core, xx, ids)
        def _(zz, q, r, c, usable):
            h = hidden_value(gate[r + t * rows], up[r + t * rows])
            got = lax.dot_general(h, cot[c], (((0,), (0,)), ((), ())), preferred_element_type=jnp.float32)
            part[core, t, xx, zz, q] = (got * (usable * scale)).astype(part.dtype)

    con_out = []

    def contribs(core, t, xx, ids):
        @slots_of(core, xx, ids)
        def _(zz, q, r, c, usable):
            got = lax.dot_general(
                cot[c], w_all[core, t, xx, zz, q], (((1,), (1,)), ((), ())), preferred_element_type=jnp.float32
            )
            con_ref[core, t, xx, zz, q] = (got * usable).astype(con_ref.dtype)

        out = pltpu.make_async_copy(con_ref.at[core, t, xx], con_hbm.at[core, t, xx], local.at[5 + len(con_out)])
        out.start()
        con_out.append(out)

    def add(dst, src):
        total = dst[...].astype(jnp.float32) + src[...].astype(jnp.float32)
        dst[...] = total.astype(dst.dtype)

    quads = ((1 - y, 1 - x, ids_other), (y, 1 - x, ids_ref), (1 - y, x, ids_other), (y, x, ids_ref))
    core_p = []

    def send_core(n):
        t, xx, ids = quads[n]
        partials(1 - k, t, xx, ids)
        core_p.append(copy(10 + n, part.at[1 - k, t, xx], rc.at[t, xx], to_core))
        core_p[n].start()

    def add_core(n):
        t, xx, _ = quads[n]
        core_p[n].wait_recv()

        @pl.loop(0, n_z)
        def _(i):
            add(part.at[k, t, xx, i], rc.at[t, xx, i])

    def own_core(n):
        t, xx, ids = quads[n]
        partials(k, t, xx, ids)

    send_core(0)
    ag_x0.wait_recv()
    ag_zx = [same(23 + d, w_all.at[k, y, 1 - x, z, :, part_rows[0]], to_z[d]) for d in range(n_z - 1)]
    ag_y1.wait_recv()
    ag_zy = [
        same(23 + n_z - 1 + d, w_all.at[k, 1 - y, x, z, :, part_rows[1]], to_z[d]) for d in range(n_z - 1)
    ]
    for c in ag_zx + ag_zy:
        c.start()
    own_core(0)
    add_core(0)
    far = part.at[k, 1 - y, 1 - x]
    rs_xa = copy(14, far.at[:, :, part_rows[0]], rx0.at[1 - y], to_x)
    rs_ya = copy(15, far.at[:, :, part_rows[1]], ry1.at[1 - x], to_y)
    rs_xa.start()
    rs_ya.start()
    send_core(1)
    own_core(1)
    send_core(2)
    add_core(1)
    rs_xb = copy(16, part.at[k, y, 1 - x, :, :, part_rows[0]], rx0.at[y], to_x)
    rs_xb.start()
    own_core(2)
    send_core(3)
    add_core(2)
    rs_yb = copy(17, part.at[k, 1 - y, x, :, :, part_rows[1]], ry1.at[x], to_y)
    rs_yb.start()
    own_core(3)

    add_core(3)

    rs_xa.wait_recv()

    @pl.loop(0, n_z)
    def _(i):
        add(part.at[k, 1 - y, x, i, :, part_rows[0]], rx0.at[1 - y, i])

    rs_y0 = copy(18, part.at[k, 1 - y, x, :, :, part_rows[0]], ry0, to_y)
    rs_y0.start()
    rs_ya.wait_recv()

    @pl.loop(0, n_z)
    def _(i):
        add(part.at[k, y, 1 - x, i, :, part_rows[1]], ry1.at[1 - x, i])

    rs_x1 = copy(19, part.at[k, y, 1 - x, :, :, part_rows[1]], rx1, to_x)
    rs_x1.start()

    for c in ag_z:
        c.wait_recv()
    mine = w_all.at[k, y, x]
    ag_ya, ag_xa = [], []
    for d in range(n_z - 1):
        came = mine.at[(z + d + 1) % n_z]
        ag_ya.append(same(37 + 2 * (n_z - 1) + d, came.at[:, part_rows[0]], to_y))
        ag_xa.append(same(37 + 3 * (n_z - 1) + d, came.at[:, part_rows[1]], to_x))
        ag_ya[d].start()
        ag_xa[d].start()
    core_w = [same(29, mine, to_core)]
    core_w[0].start()

    def to_core_w(ref):
        core_w.append(same(29 + len(core_w), ref, to_core))
        core_w[-1].start()

    contribs(k, y, x, ids_ref)
    for c in ag_zx:
        c.wait_recv()
    ag_yb = same(8, w_all.at[k, y, 1 - x, :, :, part_rows[0]], to_y)
    ag_yb.start()
    to_core_w(w_all.at[k, y, 1 - x, :, :, part_rows[0]])
    for c in ag_zy:
        c.wait_recv()
    ag_xb = same(9, w_all.at[k, 1 - y, x, :, :, part_rows[1]], to_x)
    ag_xb.start()
    to_core_w(w_all.at[k, 1 - y, x, :, :, part_rows[1]])

    rs_z = []

    def send_z(p, last, into, came, came_into):
        last.wait_recv()
        came.wait_recv()

        @pl.loop(0, n_z)
        def _(i):
            ref = part.at[k, y, x, i, :, part_rows[p]]
            total = ref[...].astype(jnp.float32) + into[i].astype(jnp.float32)
            ref[...] = (total + came_into[i].astype(jnp.float32)).astype(ref.dtype)

        for d in range(n_z - 1):
            src = part.at[k, y, x, (z + d + 1) % n_z, :, part_rows[p]]
            c = copy(37 + p * (n_z - 1) + d, src, rz.at[d, p], to_z[d])
            c.start()
            rs_z.append(c)

    send_z(0, rs_xb, rx0.at[y], rs_y0, ry0)
    send_z(1, rs_yb, ry1.at[x], rs_x1, rx1)

    core_w[0].wait_recv()
    contribs(1 - k, y, x, ids_ref)
    for c in ag_ya:
        c.wait_recv()
    to_core_w(w_all.at[k, 1 - y, x, :, :, part_rows[0]])
    contribs(k, 1 - y, x, ids_other)
    for c in ag_xa:
        c.wait_recv()
    to_core_w(w_all.at[k, y, 1 - x, :, :, part_rows[1]])
    contribs(k, y, 1 - x, ids_ref)
    for c in (core_w[2], core_w[3]):
        c.wait_recv()
    contribs(1 - k, 1 - y, x, ids_other)
    for c in (core_w[1], core_w[4]):
        c.wait_recv()
    contribs(1 - k, y, 1 - x, ids_ref)
    ag_yb.wait_recv()
    to_core_w(w_all.at[k, 1 - y, 1 - x, :, :, part_rows[0]])
    ag_xb.wait_recv()
    to_core_w(w_all.at[k, 1 - y, 1 - x, :, :, part_rows[1]])
    contribs(k, 1 - y, 1 - x, ids_other)

    for c in rs_z:
        c.wait_recv()
    for p in range(2):
        total = part[k, y, x, z, :, part_rows[p]].astype(jnp.float32)
        for d in range(n_z - 1):
            total = total + rz[d, p].astype(jnp.float32)
        wgrad_ref[0, :, part_rows[p]] = total
    for c in core_w[5:]:
        c.wait_recv()
    contribs(1 - k, 1 - y, 1 - x, ids_other)
    sent = [ids_copy, ag_x0, ag_y1, ag_xb, ag_yb, rs_xa, rs_ya, rs_xb, rs_yb, rs_x1, rs_y0]
    for c in sent + ag_z + ag_xa + ag_ya + ag_zx + ag_zy + core_p + core_w + rs_z:
        c.wait_send()
    for c in con_out:
        c.wait()


def exchange(gate, up, cot, w, ids, scale):
    tokens, ff = gate.shape
    cap, block = w.shape[1:3]
    bf16 = jnp.bfloat16
    any_spec = pl.BlockSpec(memory_space=pltpu.HBM)
    smem = pl.BlockSpec(memory_space=pltpu.SMEM)
    whole = pl.BlockSpec(memory_space=pltpu.VMEM)
    n_z = lax.axis_size("fsdp") // 4
    half = block // 2
    return pl.pallas_call(
        functools.partial(exchange_kernel, scale),
        out_shape=[
            jax.ShapeDtypeStruct(ids.shape, ids.dtype),
            jax.ShapeDtypeStruct((2, 2, 2, n_z, cap, tokens, block), bf16),
            jax.ShapeDtypeStruct(w.shape, jnp.float32),
        ],
        in_specs=[smem, any_spec, any_spec, any_spec, any_spec, any_spec],
        out_specs=[smem, any_spec, whole],
        scratch_shapes=[
            pltpu.VMEM((2, 2, 2, n_z, cap, tokens, block), bf16),
            pltpu.VMEM(ids.shape, ids.dtype),
            pltpu.VMEM((ff // block, tokens, block), bf16),
            pltpu.VMEM((ff // block, tokens, block), bf16),
            pltpu.VMEM((cot.shape[1] // block, tokens, block), bf16),
            pltpu.VMEM((2, 2, 2, n_z, cap, block, block), bf16),
            pltpu.VMEM((2, 2, 2, n_z, cap, block, block), bf16),
            pltpu.VMEM((2, 2, n_z, cap, block, block), bf16),
            pltpu.VMEM((2, n_z, cap, half, block), bf16),
            pltpu.VMEM((2, n_z, cap, half, block), bf16),
            pltpu.VMEM((n_z, cap, half, block), bf16),
            pltpu.VMEM((n_z, cap, half, block), bf16),
            pltpu.VMEM((n_z - 1, 2, cap, half, block), bf16),
            pltpu.SemaphoreType.DMA((13,)),
            pltpu.SemaphoreType.DMA((37 + 4 * (n_z - 1),)),
            pltpu.SemaphoreType.DMA((37 + 4 * (n_z - 1),)),
        ],
        compiler_params=pltpu.CompilerParams(
            collective_id=0, has_side_effects=True, vmem_limit_bytes=60 * MIB
        ),
    )(ids, ids, gate, up, cot, w)


def grads_kernel(
    cols, ids_ref, other_ref, con_hbm, wgrad_in, gate_hbm, up_hbm,
    dgate_ref, dup_ref, wgrad_out, dh_own, dh_other, con_ref, gate_ref, up_ref,
    con_sem, wgrad_sem, gate_sem, up_sem,
):
    n_z, cap, _, block = con_ref.shape[3:]
    per = dgate_ref.shape[1] // block
    y = lax.axis_index("tensor")
    step = pl.program_id(0)

    @pl.when(step == 0)
    def _():
        con_copy = pltpu.make_async_copy(con_hbm, con_ref, con_sem)
        con_copy.start()
        gate_copy = pltpu.make_async_copy(gate_hbm, gate_ref, gate_sem)
        gate_copy.start()
        up_copy = pltpu.make_async_copy(up_hbm, up_ref, up_sem)
        up_copy.start()
        pltpu.make_async_copy(wgrad_in, wgrad_out, wgrad_sem).start()
        dh_own[...] = jnp.zeros_like(dh_own)
        dh_other[...] = jnp.zeros_like(dh_other)
        con_copy.wait()
        for s in range(4 * n_z * cap):
            f = s // cap
            for t, ids, dh_ref in ((y, ids_ref, dh_own), (1 - y, other_ref, dh_other)):
                r = split_id(ids[0, s], cols)[0]
                dh_ref[r] += con_ref[f % 2, t, f // 2 % 2, f // 4, s % cap].astype(jnp.float32)
        gate_copy.wait()
        up_copy.wait()

    def apply(first, dh_ref):
        for j in range(per):
            at = slice(j * block, (j + 1) * block)
            here = pl.ds(pl.multiple_of((step * per + j) * block, block), block)
            gate_f = gate_ref[:, here].astype(jnp.float32)
            dh = dh_ref[first + j]
            sig = sigmoid(gate_f)
            silu = gate_f * sig
            dup_ref[:, at] = (dh * silu).astype(dup_ref.dtype)
            slope = sig + silu * (1.0 - sig)
            dgate_ref[:, at] = (dh * up_ref[:, here].astype(jnp.float32) * slope).astype(dgate_ref.dtype)

    half_steps = pl.num_programs(0) // 2
    first = step % half_steps * per

    @pl.when(step // half_steps == y)
    def _():
        apply(first, dh_own)

    @pl.when(step // half_steps != y)
    def _():
        apply(first, dh_other)

    @pl.when(step == pl.num_programs(0) - 1)
    def _():
        pltpu.make_async_copy(wgrad_in, wgrad_out, wgrad_sem).wait()


def local_grads(ids, other, contrib, w_grad, cols, gate, up):
    tokens, ff = gate.shape
    steps = 8
    width = ff // steps
    block = contrib.shape[-1]
    smem = pl.BlockSpec(memory_space=pltpu.SMEM)
    hbm = pl.BlockSpec(memory_space=pltpu.HBM)
    tile = pl.BlockSpec((tokens, width), lambda i: (0, i))
    return pl.pallas_call(
        functools.partial(grads_kernel, cols),
        grid=(steps,),
        out_shape=[jax.ShapeDtypeStruct(gate.shape, jnp.bfloat16)] * 2
        + [jax.ShapeDtypeStruct(w_grad.shape, w_grad.dtype)],
        in_specs=[smem, smem, hbm, hbm, hbm, hbm],
        out_specs=[tile, tile, hbm],
        scratch_shapes=[
            pltpu.VMEM((ff // block // 2, tokens, block), jnp.float32),
            pltpu.VMEM((ff // block // 2, tokens, block), jnp.float32),
            pltpu.VMEM(contrib.shape, contrib.dtype),
            pltpu.VMEM(gate.shape, gate.dtype),
            pltpu.VMEM(up.shape, up.dtype),
            pltpu.SemaphoreType.DMA,
            pltpu.SemaphoreType.DMA,
            pltpu.SemaphoreType.DMA,
            pltpu.SemaphoreType.DMA,
        ],
        compiler_params=pltpu.CompilerParams(vmem_limit_bytes=60 * MIB),
    )(ids, other, contrib, w_grad, gate, up)


def body(gate_pre, up_pre, cotangent, w_slots, slot_ids):
    scale = 1.0 / math.sqrt(cotangent.shape[0] * lax.axis_size("fsdp"))
    other, contrib, w_grad = exchange(gate_pre, up_pre, cotangent, w_slots, slot_ids, scale)
    cols = cotangent.shape[1] // w_slots.shape[2]
    return tuple(local_grads(slot_ids, other, contrib, w_grad, cols, gate_pre, up_pre))


def solution(mesh):
    placed = (
        P(("fsdp", "tensor"), None),
        P(("fsdp", "tensor"), None),
        P("fsdp", None),
        P("tensor", "fsdp", None, None),
        P("tensor", None),
    )
    small = mesh.shape["tensor"] == 2 and mesh.shape["fsdp"] == 16
    return jax.shard_map(
        body if small else wide_body,
        mesh=mesh,
        in_specs=placed,
        out_specs=(
            P(("fsdp", "tensor"), None),
            P(("fsdp", "tensor"), None),
            P("tensor", "fsdp", None, None),
        ),
        check_vma=False,
    )
```
